512 devices in a mesh: dp: 4 (over y), wide: 64 (over z, x), mp: 2 (over core).
Axes of the slice: x: 4, y: 4, z: 16, core: 2. Of those that a mesh axis runs over, the one named last changes fastest.
Arguments:
- neighbour_rows: bfloat16 [2048, 16, 896], P(('dp', 'wide')), parts along dimension 0, may hold values from -6 to 6
- lengths: int32 [2048], P('dp'), parts along dimension 0, may hold values from 1 to 16
- block_rows: int32 [1024, 2], P('dp'), parts along dimension 0, may hold values from 0 to 511, as said below
- queries: bfloat16 [65536, 2048], P(('dp', 'wide'), 'mp'), parts along dimension 0
- encoder_gain: float32 [896], replicated, may hold values from 0.1 to 1.9
- weight_in: bfloat16 [896, 1792], P('wide', 'mp'), may hold values from -0.1875 to 0.1875
- weight_out: bfloat16 [1792, 896], P('mp', 'wide'), may hold values from -0.125 to 0.125
- weight_key: bfloat16 [896, 2048], P('wide', 'mp'), may hold values from -0.1875 to 0.1875
- weight_value: bfloat16 [896, 2048], P('wide', 'mp'), may hold values from -0.1875 to 0.1875
Outputs:
- attended: bfloat16 [65536, 2048], P(('dp', 'wide'), 'mp'), parts along dimension 0
The draws below stay inside these ranges and needn't reach their ends.
There are 4 independent parts, one for each index of `dp`. The reference program is written for one: setup_inputs(seed, part) draws one part's arguments, and reference() takes and returns one part's arrays. A program takes and returns all parts, laid end to end along the dimension named above; an argument that names none is the same for every part. Nothing has to cross between parts.
Inputs may be any that keep to these rules, and one draw needn't show every extreme that they name: `block_rows`: every neighbour of the part is listed exactly once. The neighbours of one index i of wide (rows i * 8 to (i + 1) * 8 - 1) are listed by the blocks of exactly 8 indices j of wide (blocks j * 4 to (j + 1) * 4 - 1), exactly 1 times by those of each.
All inputs are finite; a program needn't handle non-finite values.
Results may differ from the reference program's by a relative error of at most 0.013.
Values may be sent and summed in bfloat16 or wider, within the bound.
A program may use at most 64 MiB of HBM per device.

```python
import jax
import jax.numpy as jnp
from jax import lax

E = 896
HD = 128
BLOCK_LEN = 64
NEIGHBOURS = 2
FFE = 1792
HEADS = 16
NLEN = 16
ROWS_DEV = 8
ROWS = 512
BLOCKS = 256
TOKENS = 16384
HQ = 2048
GROUPS = 8
CAP = 1
N_WIDE = 64


def draw_block_rows(key, part):
    key = jax.random.fold_in(key, 7)
    first_key, second_key, third_key = jax.random.split(key, 3)
    offsets = jax.random.permutation(first_key, N_WIDE)[:GROUPS].astype(jnp.int32)
    host_order = jax.vmap(lambda sub_key: jax.random.permutation(sub_key, ROWS_DEV))(jax.random.split(second_key, N_WIDE)).astype(jnp.int32)
    owners = jnp.arange(N_WIDE, dtype=jnp.int32)
    hosts = (owners[:, None] - offsets[None, :]) % N_WIDE
    local_index = jnp.arange(GROUPS, dtype=jnp.int32)[:, None] * CAP + jnp.arange(CAP, dtype=jnp.int32)[None, :]
    picked = host_order[hosts[:, :, None], local_index[None, :, :]]
    row_ids = (hosts[:, :, None] * ROWS_DEV + picked).reshape(N_WIDE, GROUPS * CAP)
    shuffle = jax.vmap(lambda sub_key: jax.random.permutation(sub_key, GROUPS * CAP))(jax.random.split(third_key, N_WIDE)).astype(jnp.int32)
    row_ids = jnp.take_along_axis(row_ids, shuffle, axis=1)
    return row_ids.reshape(BLOCKS, NEIGHBOURS).astype(jnp.int32)


def draw_queries(key, part):
    key = jax.random.fold_in(key, 11)
    first_key = jax.random.fold_in(key, 0)
    values = jax.random.normal(first_key, (TOKENS, HQ), jnp.float32)
    return values.astype(jnp.bfloat16)


def set_ends(result, stream_key, smallest, largest):
    extent = result.shape
    place = [jax.random.randint(jax.random.fold_in(stream_key, axis), (), 0, extent[axis]) for axis in range(len(extent))]
    result = result.at[tuple(place)].set(smallest)
    longest = extent.index(max(extent))
    place[longest] = (place[longest] + 1) % extent[longest]
    return result.at[tuple(place)].set(largest)


def steps_of(rng, extent, cuts, low, top_value):
    factor_of = 1.0
    for axis_at, shards_of in cuts:
        heights = jax.random.uniform(jax.random.fold_in(jax.random.fold_in(rng, 6), axis_at), (shards_of,), jnp.float32, low / len(cuts), top_value / len(cuts))
        factor_of = factor_of * jnp.repeat(jnp.exp(heights), extent[axis_at] // shards_of).reshape((-1,) + (1,) * (len(extent) - 1 - axis_at))
    return factor_of


def centred(rng, dims, width, reach, cuts=(), kind=jnp.bfloat16):
    result = jax.random.normal(rng, dims, jnp.float32) * width
    if len(cuts) > 0:
        result = steps_of(rng, dims, cuts, -0.22, 0.18) * result
    return jnp.clip(result, min=-reach, max=reach).astype(kind)


def setup_inputs(seed: int = 0, part: int = 0) -> dict:
    keys = jax.random.split(jax.random.key(seed), 10)
    own_keys = jax.random.split(jax.random.fold_in(keys[9], part), 10)
    return {
        "neighbour_rows": centred(own_keys[0], (ROWS, NLEN, E), 1.0, 6.0, ((0, 64),)),
        "lengths": set_ends(jax.random.randint(own_keys[1], (ROWS,), 1, NLEN + 1), jax.random.fold_in(own_keys[1], 1), 1, NLEN).astype(jnp.int32),
        "block_rows": draw_block_rows(jax.random.fold_in(jax.random.fold_in(keys[9], part), 71), part),
        "queries": draw_queries(jax.random.fold_in(jax.random.fold_in(keys[9], part), 71), part),
        "encoder_gain": jnp.clip(1.0 + 0.18 * jax.random.normal(keys[4], (E,), jnp.float32), 0.1, 1.9),
        "weight_in": centred(keys[5], (E, FFE), E ** -0.5, 0.1875, ((0, 64), (1, 2))),
        "weight_out": centred(keys[6], (FFE, E), FFE ** -0.5, 0.125, ((0, 2), (1, 64))),
        "weight_key": centred(keys[7], (E, HQ), E ** -0.5, 0.1875, ((0, 64), (1, 2))),
        "weight_value": centred(keys[8], (E, HQ), E ** -0.5, 0.1875, ((0, 64), (1, 2))),
    }


def encode(neighbour_rows, encoder_gain, weight_in, weight_out):
    inputs = neighbour_rows.reshape(ROWS * NLEN, E).astype(jnp.float32)
    squares = lax.optimization_barrier(jnp.mean(inputs * inputs, axis=-1, keepdims=True))
    normed = (inputs * lax.rsqrt(squares + 1e-06) * encoder_gain).astype(jnp.bfloat16)
    preact = jnp.dot(normed, weight_in, preferred_element_type=jnp.float32)
    hidden = jax.nn.gelu(preact).astype(jnp.bfloat16)
    mixed = jnp.dot(hidden, weight_out, preferred_element_type=jnp.float32)
    return (inputs + mixed).astype(jnp.bfloat16)

def attend(query_blocks, key_blocks, value_blocks, usable):
    scores = jnp.einsum('cqhd,ckhd->chqk', query_blocks.astype(jnp.float32), key_blocks.astype(jnp.float32))
    scores = scores * HD ** (-0.5)
    scores = jnp.where(usable[:, None, None, :], scores, -1e+30)
    highest = lax.optimization_barrier(jnp.max(scores, axis=-1, keepdims=True))
    powers = jnp.exp(scores - highest)
    weights = (powers / lax.optimization_barrier(jnp.sum(powers, axis=-1, keepdims=True))).astype(jnp.bfloat16)
    attended = jnp.einsum('chqk,ckhd->cqhd', weights.astype(jnp.float32), value_blocks.astype(jnp.float32))
    return attended.astype(jnp.bfloat16)

def reference(neighbour_rows, lengths, block_rows, queries, encoder_gain, weight_in, weight_out, weight_key, weight_value):
    encoded = encode(neighbour_rows, encoder_gain, weight_in, weight_out)
    key_rows = jnp.dot(encoded, weight_key, preferred_element_type=jnp.float32).astype(jnp.bfloat16)
    value_rows = jnp.dot(encoded, weight_value, preferred_element_type=jnp.float32).astype(jnp.bfloat16)
    key_rows = key_rows.reshape(ROWS, NLEN, HQ)
    value_rows = value_rows.reshape(ROWS, NLEN, HQ)
    key_blocks = key_rows[block_rows].reshape(BLOCKS, NEIGHBOURS * NLEN, HEADS, HD)
    value_blocks = value_rows[block_rows].reshape(BLOCKS, NEIGHBOURS * NLEN, HEADS, HD)
    live = lengths[block_rows]
    usable = jnp.arange(NLEN, dtype=jnp.int32)[None, None, :] < live[:, :, None]
    usable = usable.reshape(BLOCKS, NEIGHBOURS * NLEN)
    query_blocks = queries.reshape(BLOCKS, BLOCK_LEN, HEADS, HD)
    attended = attend(query_blocks, key_blocks, value_blocks, usable)
    return attended.reshape(TOKENS, HQ)
```

```python
import jax
import jax.numpy as jnp
from jax import lax
from jax.experimental import pallas as pl
from jax.experimental.pallas import tpu as pltpu
from jax.sharding import PartitionSpec as P

HD = 128
BLOCK_LEN = 64
NEIGHBOURS = 2
NY, NZ, NX = 4, 16, 4
NW = NZ * NX
MESH = pl.DeviceIdType.MESH
BF16 = jnp.bfloat16
F32 = jnp.float32
WAVES = (0, -4, 4, 8)
SPAN = (0, -1, 1, -2)


def attend(query_blocks, key_blocks, value_blocks, usable):
    scores = jnp.einsum(
        "cqhd,ckhd->chqk", query_blocks, key_blocks, preferred_element_type=jnp.float32
    )
    scores = scores * HD ** (-0.5)
    scores = jnp.where(usable[:, None, None, :], scores, -1e30)
    highest = jnp.max(scores, axis=-1, keepdims=True)
    powers = jnp.exp(scores - highest)
    weights = (powers / jnp.sum(powers, axis=-1, keepdims=True)).astype(jnp.bfloat16)
    attended = jnp.einsum(
        "chqk,ckhd->cqhd", weights, value_blocks, preferred_element_type=jnp.float32
    )
    return attended.astype(jnp.bfloat16)


def kernel(
    rows_ref, index_ref, gain_ref, ff_ref, kv_ref, key_ref, value_ref,
    ff, kv, tiles, held, sorted_rows, arrived, mixed, other,
    ff_z1, ff_z2, ff_x, ff_xf, kv_z1, kv_z2, kv_x, kv_xf, kv_y, kv_yf,
    ff_sent, kv_sent, y_sent, first_sent, first_recv, second_sent, second_recv,
    core_sent, core_recv,
):
    y = lax.axis_index("dp")
    me = lax.axis_index("wide")
    core = lax.axis_index("mp")
    z = me // NX
    x = me % NX
    holder = me % 2 == core

    def slot(zz, xx):
        return ((zz + 2 * NZ) % NZ) * NX + (xx + 2 * NX) % NX

    def plane(yy):
        return (yy + NY) % NY

    barrier = pltpu.get_barrier_semaphore()

    def greet(step, carry):
        pl.semaphore_signal(
            barrier, inc=1, device_id=(y, (me + step) % NW, core), device_id_type=MESH
        )
        return carry

    lax.fori_loop(1, NW, greet, 0)
    for target in ((plane(y + 1), me, core), (plane(y - 1), me, core), (y, me, 1 - core)):
        pl.semaphore_signal(barrier, inc=1, device_id=target, device_id_type=MESH)

    ff[:, pl.ds(me, 1)] = ff_ref[...][:, None]
    kv[pl.ds(y, 1), :, pl.ds(me, 1)] = kv_ref[pl.ds(y, 1)][:, :, None]
    at = lax.broadcasted_iota(jnp.int32, (128, 128), 0)
    of = lax.broadcasted_iota(jnp.int32, (128, 128), 1)
    pairs = (of == (at % 16) // 2 * 16 + at // 16 * 2 + at % 2).astype(F32).astype(BF16)
    in_pairs = jnp.dot(pairs, rows_ref[...], preferred_element_type=F32).astype(BF16)
    feature = lax.broadcasted_iota(jnp.int32, (896, 128), 0)
    lane = lax.broadcasted_iota(jnp.int32, (896, 128), 1)
    for tile in range(8):
        group = tile * 8 + lane // 16
        wanted = jnp.where(lane % 16 < 14, group * 14 + lane % 16, -1)
        pick = (feature == wanted).astype(F32).astype(BF16)
        tiles[tile] = jnp.dot(in_pairs, pick, preferred_element_type=F32).astype(BF16)

    pl.semaphore_wait(barrier, NW + 2)

    def send(src, dst, send_sem, recv_sem, target):
        pltpu.make_async_remote_copy(
            src_ref=src, dst_ref=dst, send_sem=send_sem, recv_sem=recv_sem,
            device_id=target, device_id_type=MESH,
        ).start()

    def wait(ref, sem):
        pltpu.make_async_copy(ref, ref, sem).wait()

    def first(step, carry):
        spot = (me // 2 + step) % (NW // 2)
        target = spot * 2 + core
        src = tiles.at[core * 4 + spot % 4, pl.ds(pl.multiple_of(spot // 4 * 16, 16), 16)]

        @pl.when(target == me)
        def _():
            pltpu.make_async_copy(src, held.at[me], first_recv).start()

        @pl.when(target != me)
        def _():
            send(src, held.at[me], first_sent, first_recv, (y, target, core))

        return carry

    lax.fori_loop(0, NW // 2, first, 0)

    class Ff:
        z1, z2, xs, xf, sent = ff_z1, ff_z2, ff_x, ff_xf, ff_sent

        @staticmethod
        def at(place, count=1):
            return ff.at[:, pl.ds(place, count)]

    class Kv:
        z1, z2, xs, xf, sent = kv_z1, kv_z2, kv_x, kv_xf, kv_sent

        @staticmethod
        def at(place, count=1):
            return kv.at[y, :, pl.ds(place, count)]

    def move(part, place, sem, target):
        send(part.at(place), part.at(place), part.sent, sem, target)

    def z1_send(part):
        for wave, off in ((1, 4), (2, -4), (3, 8)):
            move(part, me, part.z1.at[wave], (y, slot(z + off, x), core))

    def z2_send(part, wave):
        if wave:
            wait(part.at(0), part.z1.at[wave])
        for off in (1, -1, 2):
            move(part, slot(z + WAVES[wave], x), part.z2.at[wave], (y, slot(z + off, x), core))

    def x_send(part, wave):
        wait(part.at(0, 3), part.z2.at[wave])
        for span in SPAN:
            for off in (1, -1):
                move(
                    part, slot(z + WAVES[wave] + span, x), part.xs.at[wave],
                    (y, slot(z, x + off), core),
                )

    def xf_send(part, wave):
        wait(part.at(0, 8), part.xs.at[wave])
        for n, span in enumerate(SPAN):
            off = 1 if n < 2 else -1
            move(
                part, slot(z + WAVES[wave] + span, x - off), part.xf.at[wave],
                (y, slot(z, x + off), core),
            )

    def x_done(part, wave):
        wait(part.at(0, 4), part.xf.at[wave])

    def block(part_y, zz):
        return kv.at[part_y, :, pl.ds(slot(zz, 0), NX)]

    def y_send(wave):
        x_done(Kv, wave)
        for span in SPAN:
            for off in (1, -1):
                ref = block(y, z + WAVES[wave] + span)
                send(ref, ref, y_sent, kv_y.at[wave], (plane(y + off), me, core))

    def yf_send(wave):
        wait(kv.at[0, :, pl.ds(0, 32)], kv_y.at[wave])
        for n, span in enumerate(SPAN):
            off = 1 if n < 2 else -1
            ref = block(plane(y - off), z + WAVES[wave] + span)
            send(ref, ref, y_sent, kv_yf.at[wave], (plane(y + off), me, core))

    def y_done(wave):
        wait(kv.at[0, :, pl.ds(0, 16)], kv_yf.at[wave])

    def permute():
        @pl.when(holder)
        def _():
            wait(held, first_recv)
            rows = held[...].reshape(NW * 16, 128)

            def part(step, carry):
                start = pl.multiple_of(step * 256, 256)
                source = lax.broadcasted_iota(jnp.int32, (256, NW * 16), 1)
                pick = (index_ref[pl.ds(start, 256)] == source).astype(F32).astype(BF16)
                moved = jnp.dot(pick, rows, preferred_element_type=F32).astype(BF16)
                sorted_rows[pl.ds(step * 16, 16)] = moved.reshape(16, 16, 128)
                return carry

            lax.fori_loop(0, 4, part, 0)
            spot = me // 2
            dst = arrived.at[core * 4 + spot % 4, pl.ds(pl.multiple_of(spot // 4 * 16, 16), 16)]

            def second(step, carry):
                target = (me + step) % NW
                send(sorted_rows.at[target], dst, second_sent, second_recv, (y, target, core))
                return carry

            pltpu.make_async_copy(sorted_rows.at[me], dst, second_recv).start()
            lax.fori_loop(1, NW, second, 0)

    def swap_cores():
        wait(arrived.at[pl.ds(0, 4)], second_recv)
        half = arrived.at[pl.ds(core * 4, 4)]
        send(half, half, core_sent.at[0], core_recv.at[0], (y, me, 1 - core))

    z1_send(Kv)
    z1_send(Ff)
    z2_send(Kv, 0)
    z2_send(Ff, 0)
    x_send(Kv, 0)
    x_send(Ff, 0)
    xf_send(Kv, 0)
    z2_send(Kv, 1)
    z2_send(Kv, 2)
    z2_send(Ff, 1)
    y_send(0)
    z2_send(Ff, 2)
    x_send(Kv, 1)
    xf_send(Ff, 0)
    z2_send(Kv, 3)
    z2_send(Ff, 3)
    permute()
    x_send(Kv, 2)
    x_send(Ff, 1)
    xf_send(Kv, 1)
    x_send(Kv, 3)
    x_send(Ff, 2)
    yf_send(0)
    y_send(1)
    xf_send(Kv, 2)
    xf_send(Ff, 1)
    x_send(Ff, 3)
    swap_cores()
    y_send(2)
    xf_send(Kv, 3)
    xf_send(Ff, 2)
    yf_send(1)
    y_send(3)
    xf_send(Ff, 3)
    yf_send(2)

    wait(arrived.at[pl.ds(0, 4)], core_recv.at[0])
    inputs = jnp.concatenate([arrived[tile] for tile in range(8)], axis=1).astype(F32)
    squares = jnp.sum(inputs * inputs, axis=-1, keepdims=True) * (1.0 / 896)
    normed = (inputs * lax.rsqrt(squares + 1e-06) * gain_ref[...]).astype(BF16)
    for wave in range(4):
        x_done(Ff, wave)
    hidden = []
    for start, size in ((0, 256), (256, 256), (512, 256), (768, 128)):
        weight = ff[0, :, :, start : start + size].reshape(NW * 16, size)
        preact = jnp.dot(normed, weight, preferred_element_type=F32)
        hidden.append(jax.nn.gelu(preact).astype(BF16))
    hidden = jnp.concatenate(hidden, axis=1)
    for n in range(4):
        weight = ff[1, n * 16 : (n + 1) * 16].reshape(256, 896)
        mixed[:, n * 256 : (n + 1) * 256] = lax.dot_general(
            hidden, weight, (((1,), (1,)), ((), ())), preferred_element_type=F32
        )
    send(mixed, other, core_sent.at[1], core_recv.at[1], (y, me, 1 - core))
    yf_send(3)
    wait(other, core_recv.at[1])
    encoded = (inputs + (mixed[...] + other[...])).astype(BF16)
    unpair = (of == (at % 16) // 2 * 16 + at // 16 * 2 + at % 2).astype(F32).astype(BF16)
    encoded = jnp.dot(unpair, encoded, preferred_element_type=F32).astype(BF16)
    for wave in range(4):
        y_done(wave)
    for q in range(4):
        for n, out in ((0, key_ref), (1, value_ref)):
            weight = kv[q, n].reshape(NW * 16, 256)
            out[:, q * 256 : (q + 1) * 256] = jnp.dot(
                encoded, weight, preferred_element_type=F32
            ).astype(BF16)

    wait(ff.at[:, pl.ds(0, 63)], ff_sent)
    wait(kv.at[0, :, pl.ds(0, 63)], kv_sent)
    wait(kv.at[pl.ds(0, 3)], y_sent)

    @pl.when(holder)
    def _():
        wait(held.at[pl.ds(0, 31)], first_sent)
        wait(held.at[pl.ds(0, 63)], second_sent)

    @pl.when(jnp.logical_not(holder))
    def _():
        wait(held.at[pl.ds(0, 32)], first_sent)

    wait(arrived.at[pl.ds(0, 4)], core_sent.at[0])
    wait(mixed, core_sent.at[1])


def local(
    neighbour_rows,
    lengths,
    block_rows,
    queries,
    encoder_gain,
    weight_in,
    weight_out,
    weight_key,
    weight_value,
):
    wide_index = lax.axis_index("wide")
    rows_dev, seq_len, width = neighbour_rows.shape
    blocks_dev = queries.shape[0] // BLOCK_LEN
    heads_dev = weight_key.shape[1] // HD
    pad = ((0, 2), (0, 0))
    ff = jnp.stack([jnp.pad(weight_in, pad), jnp.pad(weight_out.T, pad)])
    kv = jnp.stack([jnp.pad(weight_key, pad), jnp.pad(weight_value, pad)])
    kv = kv.reshape(2, 16, 4, 256).transpose(2, 0, 1, 3)
    gain = jnp.pad(encoder_gain.reshape(NW, 14), ((0, 0), (0, 2))).reshape(1, NW * 16)
    index = (block_rows.reshape(-1, 1) * 2 + jnp.arange(2, dtype=jnp.int32)).reshape(-1, 1)
    dma = pltpu.SemaphoreType.DMA
    vmem = pl.BlockSpec(memory_space=pltpu.VMEM)
    keys, values = pl.pallas_call(
        kernel,
        out_shape=[jax.ShapeDtypeStruct((128, 1024), BF16)] * 2,
        in_specs=[vmem] * 5,
        out_specs=[vmem] * 2,
        scratch_shapes=[
            pltpu.VMEM((2, NW, 16, 896), BF16),
            pltpu.VMEM((4, 2, NW, 16, 256), BF16),
            pltpu.VMEM((8, 128, 128), BF16),
            pltpu.VMEM((NW, 16, 128), BF16),
            pltpu.VMEM((NW, 16, 128), BF16),
            pltpu.VMEM((8, 128, 128), BF16),
            pltpu.VMEM((128, 1024), F32),
            pltpu.VMEM((128, 1024), F32),
        ]
        + [dma((4,))] * 10
        + [dma] * 7
        + [dma((2,))] * 2,
        compiler_params=pltpu.CompilerParams(
            collective_id=0, has_side_effects=True, vmem_limit_bytes=48 * 2**20
        ),
        name="route_encode",
    )(neighbour_rows.reshape(rows_dev * seq_len, width), index, gain, ff, kv)
    key_blocks = keys.reshape(blocks_dev, NEIGHBOURS * seq_len, heads_dev, HD)
    value_blocks = values.reshape(blocks_dev, NEIGHBOURS * seq_len, heads_dev, HD)
    own_slots = lax.dynamic_slice_in_dim(
        block_rows, wide_index * blocks_dev, blocks_dev, 0
    ).reshape(-1)
    own_lengths = jnp.take(lengths, own_slots).reshape(blocks_dev, NEIGHBOURS)
    usable = jnp.arange(seq_len, dtype=jnp.int32)[None, None, :] < own_lengths[:, :, None]
    usable = usable.reshape(blocks_dev, NEIGHBOURS * seq_len)
    query_blocks = queries.reshape(blocks_dev, BLOCK_LEN, heads_dev, HD)
    attended = attend(query_blocks, key_blocks, value_blocks, usable)
    return attended.reshape(blocks_dev * BLOCK_LEN, heads_dev * HD)


def solution(mesh):
    in_specs = (
        P(("dp", "wide"), None, None),
        P("dp"),
        P("dp", None),
        P(("dp", "wide"), "mp"),
        P(),
        P("wide", "mp"),
        P("mp", "wide"),
        P("wide", "mp"),
        P("wide", "mp"),
    )
    out_specs = P(("dp", "wide"), "mp")
    return jax.shard_map(local, mesh=mesh, in_specs=in_specs, out_specs=out_specs, check_vma=False)
```

```python
import jax
import jax.numpy as jnp
from jax import lax
from jax.experimental import pallas as pl
from jax.experimental.pallas import tpu as pltpu
from jax.sharding import PartitionSpec as P

HD = 128
BLOCK_LEN = 64
NEIGHBOURS = 2
NY, NZ, NX = 4, 16, 4
NW = NZ * NX
MESH = pl.DeviceIdType.MESH
BF16 = jnp.bfloat16
F32 = jnp.float32
WAVES = (0, -4, 4, 8)


def one_hot(mask):
    return mask.astype(F32).astype(BF16)


def kernel(
    rows_hbm, lengths_hbm, blocks_hbm, queries_hbm, gain_hbm,
    in_hbm, out_hbm, key_hbm, value_hbm, attended_ref,
    ff, kv, tiles, held, sorted_rows, arrived, mixed, other, index, gain, keys, values,
    rows_ref, lengths_ref, blocks_ref, queries_ref, gain_ref, in_ref, out_ref, key_ref, value_ref,
    ff_z1, ff_z2, ff_x, ff_xf, kv_z1, kv_z2, kv_x, kv_xf, kv_y, kv_yf,
    ff_sent, kv_sent, y_sent, first_sent, first_recv, second_sent, second_recv,
    core_sent, core_recv, loaded,
):
    y = lax.axis_index("dp")
    me = lax.axis_index("wide")
    core = lax.axis_index("mp")
    z = me // NX
    x = me % NX
    holder = me % 2 == core
    side = 2 - 4 * core
    spans = (0, -1, 1, -side)

    def slot(zz, xx):
        return ((zz + 2 * NZ) % NZ) * NX + (xx + 2 * NX) % NX

    def plane(yy):
        return (yy + NY) % NY

    loads = [
        pltpu.make_async_copy(src, dst, loaded.at[n])
        for n, (src, dst) in enumerate(
            (
                (in_hbm, in_ref), (out_hbm, out_ref), (key_hbm, key_ref), (value_hbm, value_ref),
                (rows_hbm, rows_ref), (gain_hbm, gain_ref), (blocks_hbm, blocks_ref),
                (lengths_hbm, lengths_ref), (queries_hbm, queries_ref),
            )
        )
    ]
    for load in loads:
        load.start()
    barrier = pltpu.get_barrier_semaphore()

    def greet(step, carry):
        pl.semaphore_signal(
            barrier, inc=1, device_id=(y, (me + step) % NW, core), device_id_type=MESH
        )
        return carry

    lax.fori_loop(1, NW, greet, 0)
    for target in ((plane(y + 1), me, core), (plane(y - 1), me, core), (y, me, 1 - core)):
        pl.semaphore_signal(barrier, inc=1, device_id=target, device_id_type=MESH)

    for load in loads[:4]:
        load.wait()
    row = lax.broadcasted_iota(jnp.int32, (16, 14), 0)
    pad = one_hot(row == lax.broadcasted_iota(jnp.int32, (16, 14), 1))

    def padded(shard):
        return jnp.dot(pad, shard, preferred_element_type=F32).astype(BF16)

    ff[0, pl.ds(me, 1)] = padded(in_ref[...])[None]
    ff[1, pl.ds(me, 1)] = padded(out_ref[...])[None]
    for n, ref in ((0, key_ref), (1, value_ref)):
        shard = padded(ref[:, pl.ds(pl.multiple_of(y * 256, 256), 256)])
        kv[pl.ds(y, 1), n, pl.ds(me, 1)] = shard[None, None]

    pl.semaphore_wait(barrier, NW + 2)

    def prepare():
        for load in loads[4:8]:
            load.wait()
        at = lax.broadcasted_iota(jnp.int32, (128, 128), 0)
        of = lax.broadcasted_iota(jnp.int32, (128, 128), 1)
        pairs = one_hot(of == (at % 16) // 2 * 16 + at // 16 * 2 + at % 2)
        in_pairs = jnp.dot(pairs, rows_ref[...], preferred_element_type=F32).astype(BF16)
        feature = lax.broadcasted_iota(jnp.int32, (896, 128), 0)
        lane = lax.broadcasted_iota(jnp.int32, (1, 128), 1)
        whole = gain_ref[...]
        high = whole.astype(BF16).astype(F32)
        middle = (whole - high).astype(BF16).astype(F32)
        low = whole - high - middle
        term = lax.broadcasted_iota(jnp.int32, (16, 896), 0)
        terms = jnp.where(
            term == 0, high, jnp.where(term == 1, middle, jnp.where(term == 2, low, 0.0))
        ).astype(BF16)
        for tile in range(8):
            wanted = jnp.where(
                lane % 16 < 14, (tile * 8 + lane // 16) * 14 + lane % 16, -1
            )
            pick = one_hot(feature == wanted)
            tiles[tile] = jnp.dot(in_pairs, pick, preferred_element_type=F32).astype(BF16)
            gain[:, tile * 128 : (tile + 1) * 128] = jnp.sum(
                jnp.dot(terms, pick, preferred_element_type=F32), axis=0, keepdims=True
            )

    def number():
        listed = blocks_ref[...]
        block = lax.broadcasted_iota(jnp.int32, (NW * 16, 256), 1)
        place = lax.broadcasted_iota(jnp.int32, (NW * 16, 256), 0)
        spread = one_hot(block == place // 4)
        halves = []
        for value in (listed // 2, listed % 2):
            value = jnp.broadcast_to(value[:, None], (NEIGHBOURS, 8, 256)).reshape(16, 256)
            halves.append(
                lax.dot_general(
                    spread, value.astype(F32).astype(BF16), (((1,), (1,)), ((), ())),
                    preferred_element_type=F32,
                )
            )
        both = 4.0 * halves[0] + 2.0 * halves[1]
        place = lax.broadcasted_iota(jnp.int32, (NW * 16, 1), 0)
        half = (place % 2).astype(F32)
        index[...] = jnp.where(place // 2 % 2 == 0, both[:, 0:1], both[:, 8:9]) + half

    def send(src, dst, send_sem, recv_sem, target):
        pltpu.make_async_remote_copy(
            src_ref=src, dst_ref=dst, send_sem=send_sem, recv_sem=recv_sem,
            device_id=target, device_id_type=MESH,
        ).start()

    def wait(ref, sem):
        pltpu.make_async_copy(ref, ref, sem).wait()

    def first(step, carry):
        spot = (me // 2 + step) % (NW // 2)
        target = spot * 2 + core
        src = tiles.at[core * 4 + spot % 4, pl.ds(pl.multiple_of(spot // 4 * 16, 16), 16)]

        @pl.when(target == me)
        def _():
            pltpu.make_async_copy(src, held.at[me], first_recv).start()

        @pl.when(target != me)
        def _():
            send(src, held.at[me], first_sent, first_recv, (y, target, core))

        return carry

    def route():
        lax.fori_loop(0, NW // 2, first, 0)


    class Ff:
        z1, z2, xs, xf, sent = ff_z1, ff_z2, ff_x, ff_xf, ff_sent

        @staticmethod
        def at(place, count=1):
            return ff.at[:, pl.ds(place, count)]

    class Kv:
        z1, z2, xs, xf, sent = kv_z1, kv_z2, kv_x, kv_xf, kv_sent

        @staticmethod
        def at(place, count=1):
            return kv.at[y, :, pl.ds(place, count)]

    def move(part, place, sem, target):
        send(part.at(place), part.at(place), part.sent, sem, target)

    def z1_send(part):
        for wave, off in ((1, 4), (2, -4), (3, 8)):
            move(part, me, part.z1.at[wave], (y, slot(z + off, x), core))

    def z2_send(part, wave):
        if wave:
            wait(part.at(0), part.z1.at[wave])
        for off in (1, -1, side):
            move(part, slot(z + WAVES[wave], x), part.z2.at[wave], (y, slot(z + off, x), core))

    def x_send(part, wave):
        wait(part.at(0, 3), part.z2.at[wave])
        for span in spans:
            for off in (1, -1):
                move(
                    part, slot(z + WAVES[wave] + span, x), part.xs.at[wave],
                    (y, slot(z, x + off), core),
                )

    def xf_send(part, wave):
        wait(part.at(0, 8), part.xs.at[wave])
        for n, span in enumerate(spans):
            off = 1 if n < 2 else -1
            move(
                part, slot(z + WAVES[wave] + span, x - off), part.xf.at[wave],
                (y, slot(z, x + off), core),
            )

    def x_done(part, wave):
        wait(part.at(0, 4), part.xf.at[wave])

    def block(part_y, zz):
        return kv.at[part_y, :, pl.ds(slot(zz, 0), NX)]

    def y_send(wave):
        x_done(Kv, wave)
        for span in spans:
            for off in (1, -1):
                ref = block(y, z + WAVES[wave] + span)
                send(ref, ref, y_sent, kv_y.at[wave], (plane(y + off), me, core))

    def yf_send(wave):
        wait(kv.at[0, :, pl.ds(0, 32)], kv_y.at[wave])
        for n, span in enumerate(spans):
            off = 1 if n < 2 else -1
            ref = block(plane(y - off), z + WAVES[wave] + span)
            send(ref, ref, y_sent, kv_yf.at[wave], (plane(y + off), me, core))

    def y_done(wave):
        wait(kv.at[0, :, pl.ds(0, 16)], kv_yf.at[wave])

    def permute():
        number()

        @pl.when(holder)
        def _():
            wait(held, first_recv)
            rows = held[...].reshape(NW * 16, 128)

            def part(step, carry):
                start = pl.multiple_of(step * 256, 256)
                source = lax.broadcasted_iota(jnp.int32, (256, NW * 16), 1).astype(F32)
                pick = one_hot(index[pl.ds(start, 256)] == source)
                moved = jnp.dot(pick, rows, preferred_element_type=F32).astype(BF16)
                sorted_rows[pl.ds(step * 16, 16)] = moved.reshape(16, 16, 128)
                return carry

            lax.fori_loop(0, 4, part, 0)
            spot = me // 2
            dst = arrived.at[core * 4 + spot % 4, pl.ds(pl.multiple_of(spot // 4 * 16, 16), 16)]

            def second(step, carry):
                target = (me + step) % NW
                send(sorted_rows.at[target], dst, second_sent, second_recv, (y, target, core))
                return carry

            pltpu.make_async_copy(sorted_rows.at[me], dst, second_recv).start()
            lax.fori_loop(1, NW, second, 0)

    def swap_cores():
        wait(arrived.at[pl.ds(0, 4)], second_recv)
        half = arrived.at[pl.ds(core * 4, 4)]
        send(half, half, core_sent.at[0], core_recv.at[0], (y, me, 1 - core))

    z2_send(Kv, 0)
    z2_send(Ff, 0)
    prepare()
    route()
    z1_send(Kv)
    z1_send(Ff)
    x_send(Kv, 0)
    x_send(Ff, 0)
    xf_send(Kv, 0)
    z2_send(Kv, 1)
    z2_send(Kv, 2)
    y_send(0)
    z2_send(Kv, 3)
    x_send(Kv, 1)
    z2_send(Ff, 1)
    xf_send(Ff, 0)
    z2_send(Ff, 2)
    x_send(Kv, 2)
    xf_send(Kv, 1)
    z2_send(Ff, 3)
    x_send(Ff, 1)
    yf_send(0)
    y_send(1)
    permute()
    x_send(Kv, 3)
    xf_send(Kv, 2)
    xf_send(Ff, 1)
    x_send(Ff, 2)
    y_send(2)
    yf_send(1)
    xf_send(Kv, 3)
    x_send(Ff, 3)
    xf_send(Ff, 2)
    swap_cores()
    y_send(3)
    xf_send(Ff, 3)
    yf_send(2)

    wait(arrived.at[pl.ds(0, 4)], core_recv.at[0])
    inputs = jnp.concatenate([arrived[tile] for tile in range(8)], axis=1).astype(F32)
    squares = jnp.sum(inputs * inputs, axis=-1, keepdims=True) * (1.0 / 896)
    normed = (inputs * lax.rsqrt(squares + 1e-06) * gain[...]).astype(BF16)
    for wave in range(4):
        x_done(Ff, wave)
    hidden = []
    for start, size in ((0, 256), (256, 256), (512, 256), (768, 128)):
        weight = ff[0, :, :, start : start + size].reshape(NW * 16, size)
        preact = jnp.dot(normed, weight, preferred_element_type=F32)
        hidden.append(jax.nn.gelu(preact).astype(BF16))
    hidden = jnp.concatenate(hidden, axis=1)
    for n in range(4):
        weight = ff[1, n * 16 : (n + 1) * 16].reshape(256, 896)
        mixed[:, n * 256 : (n + 1) * 256] = lax.dot_general(
            hidden, weight, (((1,), (1,)), ((), ())), preferred_element_type=F32
        )
    send(mixed, other, core_sent.at[1], core_recv.at[1], (y, me, 1 - core))
    yf_send(3)
    wait(other, core_recv.at[1])
    encoded = (inputs + (mixed[...] + other[...])).astype(BF16)
    for wave in range(4):
        y_done(wave)
    for q in range(4):
        for n, out in ((0, keys), (1, values)):
            weight = kv[q, n].reshape(NW * 16, 256)
            out[:, q * 256 : (q + 1) * 256] = jnp.dot(
                encoded, weight, preferred_element_type=F32
            ).astype(BF16)

    loads[8].wait()
    mine = index[pl.ds(pl.multiple_of(me * 16, 16), 16)]
    source = lax.broadcasted_iota(jnp.int32, (16, 512), 1).astype(F32) * 2.0
    hit = (mine == source) | (mine == source + 1.0)
    live = jnp.where(hit, lengths_ref[...].astype(F32), 0.0)
    live = jnp.sum(live, axis=1, keepdims=True)
    lane = lax.broadcasted_iota(jnp.int32, (16, 128), 1)
    spot = lax.broadcasted_iota(jnp.int32, (16, 128), 0)
    live = jnp.sum(jnp.where(lane % 16 == spot, live, 0.0), axis=0, keepdims=True)
    lane = lax.broadcasted_iota(jnp.int32, (256, 128), 1)
    block_at = lax.broadcasted_iota(jnp.int32, (256, 128), 0) // BLOCK_LEN
    token = (lane // 16 * 2 + lane % 2).astype(F32)
    usable = (block_at == lane % 16 // 4) & (token < live)
    for head in range(8):
        part = slice(head * HD, (head + 1) * HD)
        scores = lax.dot_general(
            queries_ref[:, part], keys[:, part], (((1,), (1,)), ((), ())),
            preferred_element_type=F32,
        )
        scores = jnp.where(usable, scores * HD ** (-0.5), -1e30)
        powers = jnp.exp(scores - jnp.max(scores, axis=-1, keepdims=True))
        weights = (powers / jnp.sum(powers, axis=-1, keepdims=True)).astype(BF16)
        attended_ref[:, part] = jnp.dot(
            weights, values[:, part], preferred_element_type=F32
        ).astype(BF16)

    wait(ff.at[:, pl.ds(0, 63)], ff_sent)
    wait(kv.at[0, :, pl.ds(0, 63)], kv_sent)
    wait(kv.at[pl.ds(0, 3)], y_sent)

    @pl.when(holder)
    def _():
        wait(held.at[pl.ds(0, 31)], first_sent)
        wait(held.at[pl.ds(0, 63)], second_sent)

    @pl.when(jnp.logical_not(holder))
    def _():
        wait(held.at[pl.ds(0, 32)], first_sent)

    wait(arrived.at[pl.ds(0, 4)], core_sent.at[0])
    wait(mixed, core_sent.at[1])


def local(
    neighbour_rows,
    lengths,
    block_rows,
    queries,
    encoder_gain,
    weight_in,
    weight_out,
    weight_key,
    weight_value,
):
    dma = pltpu.SemaphoreType.DMA
    vmem = pl.BlockSpec(memory_space=pltpu.VMEM)
    return pl.pallas_call(
        kernel,
        out_shape=jax.ShapeDtypeStruct(queries.shape, BF16),
        in_specs=[pl.BlockSpec(memory_space=pl.ANY)] * 9,
        out_specs=vmem,
        scratch_shapes=[
            pltpu.VMEM((2, NW, 16, 896), BF16),
            pltpu.VMEM((4, 2, NW, 16, 256), BF16),
            pltpu.VMEM((8, 128, 128), BF16),
            pltpu.VMEM((NW, 16, 128), BF16),
            pltpu.VMEM((NW, 16, 128), BF16),
            pltpu.VMEM((8, 128, 128), BF16),
            pltpu.VMEM((128, 1024), F32),
            pltpu.VMEM((128, 1024), F32),
            pltpu.VMEM((NW * 16, 1), F32),
            pltpu.VMEM((1, NW * 16), F32),
            pltpu.VMEM((128, 1024), BF16),
            pltpu.VMEM((128, 1024), BF16),
            pltpu.VMEM((128, 896), BF16),
            pltpu.VMEM((1, 512), jnp.int32),
            pltpu.VMEM((2, 256), jnp.int32),
            pltpu.VMEM((256, 1024), BF16),
            pltpu.VMEM((1, 896), F32),
            pltpu.VMEM((14, 896), BF16),
            pltpu.VMEM((14, 896), BF16),
            pltpu.VMEM((14, 1024), BF16),
            pltpu.VMEM((14, 1024), BF16),
        ]
        + [dma((4,))] * 10
        + [dma] * 7
        + [dma((2,))] * 2
        + [dma((9,))],
        compiler_params=pltpu.CompilerParams(
            collective_id=0, has_side_effects=True, vmem_limit_bytes=60 * 2**20
        ),
        name="route_encode_attend",
    )(
        neighbour_rows.reshape(-1, neighbour_rows.shape[-1]),
        lengths.reshape(1, -1),
        block_rows.T,
        queries,
        encoder_gain.reshape(1, -1),
        weight_in,
        weight_out.T,
        weight_key,
        weight_value,
    )


def solution(mesh):
    in_specs = (
        P(("dp", "wide"), None, None),
        P("dp"),
        P("dp", None),
        P(("dp", "wide"), "mp"),
        P(),
        P("wide", "mp"),
        P("mp", "wide"),
        P("wide", "mp"),
        P("wide", "mp"),
    )
    out_specs = P(("dp", "wide"), "mp")
    return jax.shard_map(local, mesh=mesh, in_specs=in_specs, out_specs=out_specs, check_vma=False)
```

```python
import jax
import jax.numpy as jnp
from jax import lax
from jax.experimental import pallas as pl
from jax.experimental.pallas import tpu as pltpu
from jax.sharding import PartitionSpec as P

HD = 128
BLOCK_LEN = 64
NEIGHBOURS = 2
NY, NZ, NX = 4, 16, 4
NW = NZ * NX
MESH = pl.DeviceIdType.MESH
BF16 = jnp.bfloat16
F32 = jnp.float32
WAVES = (0, -4, 4, 8)


def one_hot(mask):
    return mask.astype(F32).astype(BF16)


def kernel(
    rows_hbm, lengths_hbm, blocks_hbm, queries_hbm, gain_hbm,
    in_hbm, out_hbm, key_hbm, value_hbm, attended_ref,
    ff, kv, tiles, held, sorted_rows, arrived, mixed, other, index, gain, keys, values,
    rows_ref, lengths_ref, blocks_ref, queries_ref, gain_ref, in_ref, out_ref, key_ref, value_ref,
    ff_z1, ff_z2, ff_x, ff_xf, kv_z1, kv_z2, kv_x, kv_xf, kv_y, kv_yf,
    ff_sent, kv_sent, y_sent, first_sent, first_recv, second_sent, second_recv,
    core_sent, core_recv, loaded,
):
    y = lax.axis_index("dp")
    me = lax.axis_index("wide")
    core = lax.axis_index("mp")
    z = me // NX
    x = me % NX
    holder = me % 2 == core
    side = 2 - 4 * core
    spans = (0, -1, 1, -side)

    def slot(zz, xx):
        return ((zz + 2 * NZ) % NZ) * NX + (xx + 2 * NX) % NX

    def plane(yy):
        return (yy + NY) % NY

    loads = [
        pltpu.make_async_copy(src, dst, loaded.at[n])
        for n, (src, dst) in enumerate(
            (
                (in_hbm, in_ref), (out_hbm, out_ref), (key_hbm, key_ref), (value_hbm, value_ref),
                (rows_hbm, rows_ref), (gain_hbm, gain_ref), (blocks_hbm, blocks_ref),
                (lengths_hbm, lengths_ref), (queries_hbm, queries_ref),
            )
        )
    ]
    for load in loads:
        load.start()
    barrier = pltpu.get_barrier_semaphore()

    def greet(step, carry):
        pl.semaphore_signal(
            barrier, inc=1, device_id=(y, (me + step) % NW, core), device_id_type=MESH
        )
        return carry

    lax.fori_loop(1, NW, greet, 0)
    for target in ((plane(y + 1), me, core), (plane(y - 1), me, core), (y, me, 1 - core)):
        pl.semaphore_signal(barrier, inc=1, device_id=target, device_id_type=MESH)

    for load in loads[:4]:
        load.wait()
    row = lax.broadcasted_iota(jnp.int32, (16, 14), 0)
    pad = one_hot(row == lax.broadcasted_iota(jnp.int32, (16, 14), 1))

    def padded(shard):
        return jnp.dot(pad, shard, preferred_element_type=F32).astype(BF16)

    ff[0, pl.ds(me, 1)] = padded(in_ref[...])[None]
    ff[1, pl.ds(me, 1)] = padded(out_ref[...])[None]
    for n, ref in ((0, key_ref), (1, value_ref)):
        shard = padded(ref[:, pl.ds(pl.multiple_of(y * 256, 256), 256)])
        kv[pl.ds(y, 1), n, pl.ds(me, 1)] = shard[None, None]

    pl.semaphore_wait(barrier, NW + 2)

    def prepare():
        for load in loads[4:8]:
            load.wait()
        at = lax.broadcasted_iota(jnp.int32, (128, 128), 0)
        of = lax.broadcasted_iota(jnp.int32, (128, 128), 1)
        pairs = one_hot(of == (at % 16) // 2 * 16 + at // 16 * 2 + at % 2)
        in_pairs = jnp.dot(pairs, rows_ref[...], preferred_element_type=F32).astype(BF16)
        feature = lax.broadcasted_iota(jnp.int32, (896, 128), 0)
        lane = lax.broadcasted_iota(jnp.int32, (1, 128), 1)
        whole = gain_ref[...].reshape(1, 896)
        high = whole.astype(BF16).astype(F32)
        middle = (whole - high).astype(BF16).astype(F32)
        low = whole - high - middle
        term = lax.broadcasted_iota(jnp.int32, (16, 896), 0)
        terms = jnp.where(
            term == 0, high, jnp.where(term == 1, middle, jnp.where(term == 2, low, 0.0))
        ).astype(BF16)
        for tile in range(8):
            wanted = jnp.where(
                lane % 16 < 14, (tile * 8 + lane // 16) * 14 + lane % 16, -1
            )
            pick = one_hot(feature == wanted)
            tiles[tile] = jnp.dot(in_pairs, pick, preferred_element_type=F32).astype(BF16)
            gain[:, tile * 128 : (tile + 1) * 128] = jnp.sum(
                jnp.dot(terms, pick, preferred_element_type=F32), axis=0, keepdims=True
            )

    def number():
        listed = blocks_ref[...]
        block = lax.broadcasted_iota(jnp.int32, (NW * 16, 256), 1)
        place = lax.broadcasted_iota(jnp.int32, (NW * 16, 256), 0)
        spread = one_hot(block == place // 4)
        halves = []
        for value in (listed // 2, listed % 2):
            value = jnp.broadcast_to(value[:, None], (NEIGHBOURS, 8, 256)).reshape(16, 256)
            halves.append(
                lax.dot_general(
                    spread, value.astype(F32).astype(BF16), (((1,), (1,)), ((), ())),
                    preferred_element_type=F32,
                )
            )
        both = 4.0 * halves[0] + 2.0 * halves[1]
        place = lax.broadcasted_iota(jnp.int32, (NW * 16, 1), 0)
        half = (place % 2).astype(F32)
        index[...] = jnp.where(place // 2 % 2 == 0, both[:, 0:1], both[:, 8:9]) + half

    def send(src, dst, send_sem, recv_sem, target):
        pltpu.make_async_remote_copy(
            src_ref=src, dst_ref=dst, send_sem=send_sem, recv_sem=recv_sem,
            device_id=target, device_id_type=MESH,
        ).start()

    def wait(ref, sem):
        pltpu.make_async_copy(ref, ref, sem).wait()

    def first(step, carry):
        spot = (me // 2 + step) % (NW // 2)
        target = spot * 2 + core
        src = tiles.at[core * 4 + spot % 4, pl.ds(pl.multiple_of(spot // 4 * 16, 16), 16)]

        @pl.when(target == me)
        def _():
            pltpu.make_async_copy(src, held.at[me], first_recv).start()

        @pl.when(target != me)
        def _():
            send(src, held.at[me], first_sent, first_recv, (y, target, core))

        return carry

    def route():
        lax.fori_loop(0, NW // 2, first, 0)


    class Ff:
        z1, z2, xs, xf, sent = ff_z1, ff_z2, ff_x, ff_xf, ff_sent

        @staticmethod
        def at(place, count=1):
            return ff.at[:, pl.ds(place, count)]

    class Kv:
        z1, z2, xs, xf, sent = kv_z1, kv_z2, kv_x, kv_xf, kv_sent

        @staticmethod
        def at(place, count=1):
            return kv.at[y, :, pl.ds(place, count)]

    def move(part, place, sem, target):
        send(part.at(place), part.at(place), part.sent, sem, target)

    def z1_send(part):
        for wave, off in ((1, 4), (2, -4), (3, 8)):
            move(part, me, part.z1.at[wave], (y, slot(z + off, x), core))

    def z2_send(part, wave):
        if wave:
            wait(part.at(0), part.z1.at[wave])
        for off in (1, -1, side):
            move(part, slot(z + WAVES[wave], x), part.z2.at[wave], (y, slot(z + off, x), core))

    def x_send(part, wave):
        wait(part.at(0, 3), part.z2.at[wave])
        for span in spans:
            for off in (1, -1):
                move(
                    part, slot(z + WAVES[wave] + span, x), part.xs.at[wave],
                    (y, slot(z, x + off), core),
                )

    def xf_send(part, wave):
        wait(part.at(0, 8), part.xs.at[wave])
        for n, span in enumerate(spans):
            off = 1 if n < 2 else -1
            move(
                part, slot(z + WAVES[wave] + span, x - off), part.xf.at[wave],
                (y, slot(z, x + off), core),
            )

    def x_done(part, wave):
        wait(part.at(0, 4), part.xf.at[wave])

    def block(part_y, zz):
        return kv.at[part_y, :, pl.ds(slot(zz, 0), NX)]

    def y_send(wave):
        x_done(Kv, wave)
        for span in spans:
            for off in (1, -1):
                ref = block(y, z + WAVES[wave] + span)
                send(ref, ref, y_sent, kv_y.at[wave], (plane(y + off), me, core))

    def yf_send(wave):
        wait(kv.at[0, :, pl.ds(0, 32)], kv_y.at[wave])
        for n, span in enumerate(spans):
            off = 1 if n < 2 else -1
            ref = block(plane(y - off), z + WAVES[wave] + span)
            send(ref, ref, y_sent, kv_yf.at[wave], (plane(y + off), me, core))

    def y_done(wave):
        wait(kv.at[0, :, pl.ds(0, 16)], kv_yf.at[wave])

    def permute():
        number()

        @pl.when(holder)
        def _():
            wait(held, first_recv)
            rows = held[...].reshape(NW * 16, 128)

            def part(step, carry):
                start = pl.multiple_of(step * 256, 256)
                source = lax.broadcasted_iota(jnp.int32, (256, NW * 16), 1).astype(F32)
                pick = one_hot(index[pl.ds(start, 256)] == source)
                moved = jnp.dot(pick, rows, preferred_element_type=F32).astype(BF16)
                sorted_rows[pl.ds(step * 16, 16)] = moved.reshape(16, 16, 128)
                return carry

            lax.fori_loop(0, 4, part, 0)
            spot = me // 2
            dst = arrived.at[core * 4 + spot % 4, pl.ds(pl.multiple_of(spot // 4 * 16, 16), 16)]

            def second(step, carry):
                target = (me + step) % NW
                send(sorted_rows.at[target], dst, second_sent, second_recv, (y, target, core))
                return carry

            pltpu.make_async_copy(sorted_rows.at[me], dst, second_recv).start()
            lax.fori_loop(1, NW, second, 0)

    def swap_cores():
        wait(arrived.at[pl.ds(0, 4)], second_recv)
        half = arrived.at[pl.ds(core * 4, 4)]
        send(half, half, core_sent.at[0], core_recv.at[0], (y, me, 1 - core))

    z1_send(Kv)
    z2_send(Kv, 0)
    z2_send(Ff, 0)
    z2_send(Kv, 1)
    z2_send(Kv, 2)
    x_send(Kv, 0)
    z1_send(Ff)
    x_send(Ff, 0)
    z2_send(Kv, 3)
    x_send(Kv, 2)
    prepare()
    x_send(Kv, 1)
    xf_send(Kv, 0)
    z2_send(Ff, 1)
    xf_send(Ff, 0)
    route()
    xf_send(Kv, 2)
    xf_send(Kv, 1)
    x_send(Kv, 3)
    y_send(0)
    x_send(Ff, 1)
    z2_send(Ff, 2)
    y_send(1)
    y_send(2)
    z2_send(Ff, 3)
    yf_send(0)
    xf_send(Kv, 3)
    x_send(Ff, 2)
    xf_send(Ff, 1)
    permute()
    x_send(Ff, 3)
    y_send(3)
    yf_send(1)
    yf_send(2)
    xf_send(Ff, 2)
    xf_send(Ff, 3)
    swap_cores()
    yf_send(3)

    wait(arrived.at[pl.ds(0, 4)], core_recv.at[0])
    inputs = jnp.concatenate([arrived[tile] for tile in range(8)], axis=1).astype(F32)
    squares = jnp.sum(inputs * inputs, axis=-1, keepdims=True) * (1.0 / 896)
    normed = (inputs * lax.rsqrt(squares + 1e-06) * gain[...]).astype(BF16)
    for wave in range(4):
        x_done(Ff, wave)
    hidden = []
    for start, size in ((0, 256), (256, 256), (512, 256), (768, 128)):
        weight = ff[0, :, :, start : start + size].reshape(NW * 16, size)
        preact = jnp.dot(normed, weight, preferred_element_type=F32)
        hidden.append(jax.nn.gelu(preact).astype(BF16))
    hidden = jnp.concatenate(hidden, axis=1)
    for n in range(4):
        weight = ff[1, n * 16 : (n + 1) * 16].reshape(256, 896)
        mixed[n] = lax.dot_general(
            hidden, weight, (((1,), (1,)), ((), ())), preferred_element_type=F32
        )
        send(mixed.at[n], other.at[n], core_sent.at[n + 1], core_recv.at[n + 1], (y, me, 1 - core))
    encoded = []
    for n in range(4):
        wait(other.at[n], core_recv.at[n + 1])
        part = inputs[:, n * 256 : (n + 1) * 256] + (mixed[n] + other[n])
        encoded.append(part.astype(BF16))
    encoded = jnp.concatenate(encoded, axis=1)
    for wave in range(4):
        y_done(wave)
    for q in range(4):
        for n, out in ((0, keys), (1, values)):
            weight = kv[q, n].reshape(NW * 16, 256)
            out[:, q * 256 : (q + 1) * 256] = jnp.dot(
                encoded, weight, preferred_element_type=F32
            ).astype(BF16)

    loads[8].wait()
    mine = index[pl.ds(pl.multiple_of(me * 16, 16), 16)]
    source = lax.broadcasted_iota(jnp.int32, (16, 512), 1).astype(F32) * 2.0
    hit = (mine == source) | (mine == source + 1.0)
    live = jnp.where(hit, lengths_ref[...].astype(F32), 0.0)
    live = jnp.sum(live, axis=1, keepdims=True)
    lane = lax.broadcasted_iota(jnp.int32, (16, 128), 1)
    spot = lax.broadcasted_iota(jnp.int32, (16, 128), 0)
    live = jnp.sum(jnp.where(lane % 16 == spot, live, 0.0), axis=0, keepdims=True)
    lane = lax.broadcasted_iota(jnp.int32, (256, 128), 1)
    block_at = lax.broadcasted_iota(jnp.int32, (256, 128), 0) // BLOCK_LEN
    token = (lane // 16 * 2 + lane % 2).astype(F32)
    usable = (block_at == lane % 16 // 4) & (token < live)
    for head in range(8):
        part = slice(head * HD, (head + 1) * HD)
        scores = lax.dot_general(
            queries_ref[:, part], keys[:, part], (((1,), (1,)), ((), ())),
            preferred_element_type=F32,
        )
        scores = jnp.where(usable, scores * HD ** (-0.5), -1e30)
        powers = jnp.exp(scores - jnp.max(scores, axis=-1, keepdims=True))
        weights = (powers / jnp.sum(powers, axis=-1, keepdims=True)).astype(BF16)
        attended_ref[:, part] = jnp.dot(
            weights, values[:, part], preferred_element_type=F32
        ).astype(BF16)

    wait(ff.at[:, pl.ds(0, 63)], ff_sent)
    wait(kv.at[0, :, pl.ds(0, 63)], kv_sent)
    wait(kv.at[pl.ds(0, 3)], y_sent)

    @pl.when(holder)
    def _():
        wait(held.at[pl.ds(0, 31)], first_sent)
        wait(held.at[pl.ds(0, 63)], second_sent)

    @pl.when(jnp.logical_not(holder))
    def _():
        wait(held.at[pl.ds(0, 32)], first_sent)

    wait(arrived.at[pl.ds(0, 4)], core_sent.at[0])
    for n in range(4):
        wait(mixed.at[n], core_sent.at[n + 1])


def local(
    neighbour_rows,
    lengths,
    block_rows,
    queries,
    encoder_gain,
    weight_in,
    weight_out,
    weight_key,
    weight_value,
):
    dma = pltpu.SemaphoreType.DMA
    vmem = pl.BlockSpec(memory_space=pltpu.VMEM)
    return pl.pallas_call(
        kernel,
        out_shape=jax.ShapeDtypeStruct(queries.shape, BF16),
        in_specs=[pl.BlockSpec(memory_space=pl.ANY)] * 9,
        out_specs=vmem,
        scratch_shapes=[
            pltpu.VMEM((2, NW, 16, 896), BF16),
            pltpu.VMEM((4, 2, NW, 16, 256), BF16),
            pltpu.VMEM((8, 128, 128), BF16),
            pltpu.VMEM((NW, 16, 128), BF16),
            pltpu.VMEM((NW, 16, 128), BF16),
            pltpu.VMEM((8, 128, 128), BF16),
            pltpu.VMEM((4, 128, 256), F32),
            pltpu.VMEM((4, 128, 256), F32),
            pltpu.VMEM((NW * 16, 1), F32),
            pltpu.VMEM((1, NW * 16), F32),
            pltpu.VMEM((128, 1024), BF16),
            pltpu.VMEM((128, 1024), BF16),
            pltpu.VMEM((128, 896), BF16),
            pltpu.VMEM((1, 512), jnp.int32),
            pltpu.VMEM((2, 256), jnp.int32),
            pltpu.VMEM((256, 1024), BF16),
            pltpu.VMEM((896,), F32),
            pltpu.VMEM((14, 896), BF16),
            pltpu.VMEM((14, 896), BF16),
            pltpu.VMEM((14, 1024), BF16),
            pltpu.VMEM((14, 1024), BF16),
        ]
        + [dma((4,))] * 10
        + [dma] * 7
        + [dma((5,))] * 2
        + [dma((9,))],
        compiler_params=pltpu.CompilerParams(
            collective_id=0, has_side_effects=True, vmem_limit_bytes=60 * 2**20
        ),
        name="route_encode_attend",
    )(
        neighbour_rows.reshape(-1, neighbour_rows.shape[-1]),
        lengths.reshape(1, -1),
        block_rows.T,
        queries,
        encoder_gain,
        weight_in,
        weight_out.T,
        weight_key,
        weight_value,
    )


def solution(mesh):
    in_specs = (
        P(("dp", "wide"), None, None),
        P("dp"),
        P("dp", None),
        P(("dp", "wide"), "mp"),
        P(),
        P("wide", "mp"),
        P("mp", "wide"),
        P("wide", "mp"),
        P("wide", "mp"),
    )
    out_specs = P(("dp", "wide"), "mp")
    return jax.shard_map(local, mesh=mesh, in_specs=in_specs, out_specs=out_specs, check_vma=False)
```

```python
import jax
import jax.numpy as jnp
from jax import lax
from jax.experimental import pallas as pl
from jax.experimental.pallas import tpu as pltpu
from jax.sharding import PartitionSpec as P

HD = 128
BLOCK_LEN = 64
NEIGHBOURS = 2
NY, NZ, NX = 4, 16, 4
NW = NZ * NX
MESH = pl.DeviceIdType.MESH
BF16 = jnp.bfloat16
F32 = jnp.float32
WAVES = (0, -4, 4, 8)


def one_hot(mask):
    return mask.astype(F32).astype(BF16)


def kernel(
    rows_hbm, lengths_hbm, blocks_hbm, queries_hbm, gain_hbm,
    in_hbm, out_hbm, key_hbm, value_hbm, attended_ref,
    ff, kv, tiles, held, sorted_rows, arrived, mixed, other, index, gain, keys, values,
    rows_ref, lengths_ref, blocks_ref, queries_ref, gain_ref, in_ref, out_ref, key_ref, value_ref,
    ff_z1, ff_z2, ff_x, ff_xf, kv_z1, kv_z2, kv_x, kv_xf, kv_y, kv_yf,
    ff_sent, kv_sent, y_sent, first_sent, first_recv, second_sent, second_recv,
    core_sent, core_recv, loaded, far_sent, far_recv,
):
    y = lax.axis_index("dp")
    me = lax.axis_index("wide")
    core = lax.axis_index("mp")
    z = me // NX
    x = me % NX
    holder = me % 2 == core
    side = 2 - 4 * core
    spans = (0, -1, 1, -side)

    def slot(zz, xx):
        return ((zz + 2 * NZ) % NZ) * NX + (xx + 2 * NX) % NX

    def plane(yy):
        return (yy + NY) % NY

    loads = [
        pltpu.make_async_copy(src, dst, loaded.at[n])
        for n, (src, dst) in enumerate(
            (
                (in_hbm, in_ref), (out_hbm, out_ref), (key_hbm, key_ref), (value_hbm, value_ref),
                (rows_hbm, rows_ref), (gain_hbm, gain_ref), (blocks_hbm, blocks_ref),
                (lengths_hbm, lengths_ref), (queries_hbm, queries_ref),
            )
        )
    ]
    for load in loads:
        load.start()
    barrier = pltpu.get_barrier_semaphore()

    def greet(step, carry):
        pl.semaphore_signal(
            barrier, inc=1, device_id=(y, (me + step) % NW, core), device_id_type=MESH
        )
        return carry

    lax.fori_loop(1, NW, greet, 0)
    for target in (
        (plane(y + 1), me, core), (plane(y - 1), me, core), (plane(y + 2), me, core),
        (y, me, 1 - core),
    ):
        pl.semaphore_signal(barrier, inc=1, device_id=target, device_id_type=MESH)

    for load in loads[:4]:
        load.wait()
    row = lax.broadcasted_iota(jnp.int32, (16, 14), 0)
    pad = one_hot(row == lax.broadcasted_iota(jnp.int32, (16, 14), 1))

    def padded(shard):
        return jnp.dot(pad, shard, preferred_element_type=F32).astype(BF16)

    ff[0, pl.ds(me, 1)] = padded(in_ref[...])[None]
    ff[1, pl.ds(me, 1)] = padded(out_ref[...])[None]
    for n, ref in ((0, key_ref), (1, value_ref)):
        shard = padded(ref[:, pl.ds(pl.multiple_of(y * 256, 256), 256)])
        kv[pl.ds(y, 1), n, pl.ds(me, 1)] = shard[None, None]

    pl.semaphore_wait(barrier, NW + 3)

    def prepare():
        for load in loads[4:8]:
            load.wait()
        at = lax.broadcasted_iota(jnp.int32, (128, 128), 0)
        of = lax.broadcasted_iota(jnp.int32, (128, 128), 1)
        pairs = one_hot(of == (at % 16) // 2 * 16 + at // 16 * 2 + at % 2)
        in_pairs = jnp.dot(pairs, rows_ref[...], preferred_element_type=F32).astype(BF16)
        feature = lax.broadcasted_iota(jnp.int32, (896, 128), 0)
        lane = lax.broadcasted_iota(jnp.int32, (1, 128), 1)
        exact = gain_ref[...].reshape(1, 896)
        high = exact.astype(BF16).astype(F32)
        middle = (exact - high).astype(BF16).astype(F32)
        low = exact - high - middle
        term = lax.broadcasted_iota(jnp.int32, (16, 896), 0)
        terms = jnp.where(
            term == 0, high, jnp.where(term == 1, middle, jnp.where(term == 2, low, 0.0))
        ).astype(BF16)
        for tile in range(8):
            wanted = jnp.where(
                lane % 16 < 14, (tile * 8 + lane // 16) * 14 + lane % 16, -1
            )
            pick = one_hot(feature == wanted)
            tiles[tile] = jnp.dot(in_pairs, pick, preferred_element_type=F32).astype(BF16)
            gain[:, tile * 128 : (tile + 1) * 128] = jnp.sum(
                jnp.dot(terms, pick, preferred_element_type=F32), axis=0, keepdims=True
            )

    def number():
        listed = blocks_ref[...]
        block = lax.broadcasted_iota(jnp.int32, (NW * 16, 256), 1)
        place = lax.broadcasted_iota(jnp.int32, (NW * 16, 256), 0)
        spread = one_hot(block == place // 4)
        halves = []
        for value in (listed // 2, listed % 2):
            value = jnp.broadcast_to(value[:, None], (NEIGHBOURS, 8, 256)).reshape(16, 256)
            halves.append(
                lax.dot_general(
                    spread, value.astype(F32).astype(BF16), (((1,), (1,)), ((), ())),
                    preferred_element_type=F32,
                )
            )
        both = 4.0 * halves[0] + 2.0 * halves[1]
        place = lax.broadcasted_iota(jnp.int32, (NW * 16, 1), 0)
        half = (place % 2).astype(F32)
        index[...] = jnp.where(place // 2 % 2 == 0, both[:, 0:1], both[:, 8:9]) + half

    def send(src, dst, send_sem, recv_sem, target):
        pltpu.make_async_remote_copy(
            src_ref=src, dst_ref=dst, send_sem=send_sem, recv_sem=recv_sem,
            device_id=target, device_id_type=MESH,
        ).start()

    def wait(ref, sem):
        pltpu.make_async_copy(ref, ref, sem).wait()

    def first(step, carry):
        spot = (me // 2 + step) % (NW // 2)
        target = spot * 2 + core
        src = tiles.at[core * 4 + spot % 4, pl.ds(pl.multiple_of(spot // 4 * 16, 16), 16)]

        @pl.when(target == me)
        def _():
            pltpu.make_async_copy(src, held.at[me], first_recv).start()

        @pl.when(target != me)
        def _():
            send(src, held.at[me], first_sent, first_recv, (y, target, core))

        return carry

    def route():
        lax.fori_loop(0, NW // 2, first, 0)


    class Ff:
        z1, z2, xs, xf, sent = ff_z1, ff_z2, ff_x, ff_xf, ff_sent

        @staticmethod
        def at(place, count=1):
            return ff.at[:, pl.ds(place, count)]

    class Kv:
        z1, z2, xs, xf, sent = kv_z1, kv_z2, kv_x, kv_xf, kv_sent

        @staticmethod
        def at(place, count=1):
            return kv.at[y, :, pl.ds(place, count)]

    def move(part, place, sem, target):
        send(part.at(place), part.at(place), part.sent, sem, target)

    def z1_send(wave):
        off = (4, -4, 8)[wave - 1]
        move(Kv, me, kv_z1.at[wave], (y, slot(z + off, x), core))

    turn = (y + core) % 2
    whole = y < 2
    fetched = ff_z1.at[1 + turn]

    def fetch():
        @pl.when(whole)
        def _():
            ref = ff.at[:, pl.ds(me, 1)]
            send(ref, ref, far_sent, fetched, (y, slot(z + 4 - 8 * turn, x), core))

        @pl.when(jnp.logical_not(whole))
        def _():
            ref = ff.at[y % 2, pl.ds(me, 1)]
            send(ref, ref, far_sent, far_recv, (y, slot(z + 8, x), core))

    def spread():
        @pl.when(whole)
        def _():
            wait(ff.at[:, pl.ds(0, 1)], fetched)
            ref = ff.at[:, pl.ds(slot(z - 4 + 8 * turn, x), 1)]
            for off in (1, -1, 2):
                send(ref, ref, far_sent, fetched, (plane(y + off), me, core))

        @pl.when(jnp.logical_not(whole))
        def _():
            wait(ff.at[0, pl.ds(0, 1)], far_recv)
            ref = ff.at[y % 2, pl.ds(slot(z + 8, x), 1)]
            for off in (1, -1, 2):
                send(ref, ref, far_sent, ff_z1.at[3], (plane(y + off), me, core))

    def z2_send(part, wave):
        if part is Kv and wave:
            wait(part.at(0), part.z1.at[wave])
        elif wave == 3:

            @pl.when(whole)
            def _():
                wait(ff.at[:, pl.ds(0, 1)], ff_z1.at[3])

            @pl.when(jnp.logical_not(whole))
            def _():
                wait(ff.at[0, pl.ds(0, 1)], ff_z1.at[3])
        elif wave:

            @pl.when(jnp.logical_not(whole & (turn == wave - 1)))
            def _():
                wait(ff.at[:, pl.ds(0, 1)], ff_z1.at[wave])

        for off in (1, -1, side):
            move(part, slot(z + WAVES[wave], x), part.z2.at[wave], (y, slot(z + off, x), core))

    def own_send(part, wave):
        for off in (1, -1):
            move(part, slot(z + WAVES[wave], x), part.xs.at[wave], (y, slot(z, x + off), core))

    def x_send(part, wave):
        wait(part.at(0, 3), part.z2.at[wave])
        for span in spans[1:]:
            for off in (1, -1):
                move(
                    part, slot(z + WAVES[wave] + span, x), part.xs.at[wave],
                    (y, slot(z, x + off), core),
                )

    def xf_send(part, wave):
        wait(part.at(0, 8), part.xs.at[wave])
        for n, span in enumerate(spans):
            off = 1 if n < 2 else -1
            move(
                part, slot(z + WAVES[wave] + span, x - off), part.xf.at[wave],
                (y, slot(z, x + off), core),
            )

    def x_done(part, wave):
        wait(part.at(0, 4), part.xf.at[wave])

    def block(part_y, zz):
        return kv.at[part_y, :, pl.ds(slot(zz, 0), NX)]

    def y_send(wave):
        x_done(Kv, wave)
        for span in spans:
            for off in (1, -1):
                ref = block(y, z + WAVES[wave] + span)
                send(ref, ref, y_sent, kv_y.at[wave], (plane(y + off), me, core))

    def yf_send(wave):
        wait(kv.at[0, :, pl.ds(0, 32)], kv_y.at[wave])
        for n, span in enumerate(spans):
            off = 1 if n < 2 else -1
            ref = block(plane(y - off), z + WAVES[wave] + span)
            send(ref, ref, y_sent, kv_yf.at[wave], (plane(y + off), me, core))

    def y_done(wave):
        wait(kv.at[0, :, pl.ds(0, 16)], kv_yf.at[wave])

    def permute():
        number()

        @pl.when(holder)
        def _():
            wait(held, first_recv)
            rows = held[...].reshape(NW * 16, 128)

            def part(step, carry):
                start = pl.multiple_of(step * 256, 256)
                source = lax.broadcasted_iota(jnp.int32, (256, NW * 16), 1).astype(F32)
                pick = one_hot(index[pl.ds(start, 256)] == source)
                moved = jnp.dot(pick, rows, preferred_element_type=F32).astype(BF16)
                sorted_rows[pl.ds(step * 16, 16)] = moved.reshape(16, 16, 128)
                return carry

            lax.fori_loop(0, 4, part, 0)
            spot = me // 2
            dst = arrived.at[core * 4 + spot % 4, pl.ds(pl.multiple_of(spot // 4 * 16, 16), 16)]

            def second(step, carry):
                target = (me + step) % NW
                send(sorted_rows.at[target], dst, second_sent, second_recv, (y, target, core))
                return carry

            pltpu.make_async_copy(sorted_rows.at[me], dst, second_recv).start()
            lax.fori_loop(1, NW, second, 0)

    def swap_cores():
        wait(arrived.at[pl.ds(0, 4)], second_recv)
        half = arrived.at[pl.ds(core * 4, 4)]
        send(half, half, core_sent.at[0], core_recv.at[0], (y, me, 1 - core))

    z2_send(Kv, 0)
    z1_send(1)
    z1_send(2)
    z2_send(Ff, 0)
    own_send(Ff, 0)
    own_send(Kv, 0)
    fetch()
    x_send(Kv, 0)
    prepare()
    z1_send(3)
    z2_send(Kv, 2)
    own_send(Kv, 2)
    x_send(Ff, 0)
    z2_send(Kv, 1)
    xf_send(Kv, 0)
    route()
    own_send(Kv, 1)
    x_send(Kv, 2)
    spread()
    xf_send(Ff, 0)
    z2_send(Kv, 3)
    y_send(0)
    x_send(Kv, 1)
    own_send(Kv, 3)
    xf_send(Kv, 2)
    z2_send(Ff, 1)
    x_send(Kv, 3)
    z2_send(Ff, 3)
    own_send(Ff, 3)
    xf_send(Kv, 1)
    own_send(Ff, 1)
    z2_send(Ff, 2)
    y_send(2)
    xf_send(Kv, 3)
    own_send(Ff, 2)
    x_send(Ff, 1)
    y_send(1)
    x_send(Ff, 3)
    permute()
    x_send(Ff, 2)
    y_send(3)
    yf_send(2)
    xf_send(Ff, 3)
    yf_send(0)
    xf_send(Ff, 1)
    yf_send(3)
    xf_send(Ff, 2)
    yf_send(1)
    swap_cores()

    wait(arrived.at[pl.ds(0, 4)], core_recv.at[0])
    inputs = jnp.concatenate([arrived[tile] for tile in range(8)], axis=1).astype(F32)
    squares = jnp.sum(inputs * inputs, axis=-1, keepdims=True) * (1.0 / 896)
    normed = (inputs * lax.rsqrt(squares + 1e-06) * gain[...]).astype(BF16)
    for wave in range(4):
        x_done(Ff, wave)
    hidden = []
    for start, size in ((0, 256), (256, 256), (512, 256), (768, 128)):
        weight = ff[0, :, :, start : start + size].reshape(NW * 16, size)
        preact = jnp.dot(normed, weight, preferred_element_type=F32)
        hidden.append(jax.nn.gelu(preact).astype(BF16))
    hidden = jnp.concatenate(hidden, axis=1)
    for n in range(4):
        weight = ff[1, n * 16 : (n + 1) * 16].reshape(256, 896)
        mixed[n] = lax.dot_general(
            hidden, weight, (((1,), (1,)), ((), ())), preferred_element_type=F32
        )
        send(mixed.at[n], other.at[n], core_sent.at[n + 1], core_recv.at[n + 1], (y, me, 1 - core))
    encoded = []
    for n in range(4):
        wait(other.at[n], core_recv.at[n + 1])
        part = inputs[:, n * 256 : (n + 1) * 256] + (mixed[n] + other[n])
        encoded.append(part.astype(BF16))
    encoded = jnp.concatenate(encoded, axis=1)
    for wave in range(4):
        y_done(wave)
    for q in range(4):
        for n, out in ((0, keys), (1, values)):
            weight = kv[q, n].reshape(NW * 16, 256)
            out[:, q * 256 : (q + 1) * 256] = jnp.dot(
                encoded, weight, preferred_element_type=F32
            ).astype(BF16)

    loads[8].wait()
    mine = index[pl.ds(pl.multiple_of(me * 16, 16), 16)]
    source = lax.broadcasted_iota(jnp.int32, (16, 512), 1).astype(F32) * 2.0
    hit = (mine == source) | (mine == source + 1.0)
    live = jnp.where(hit, lengths_ref[...].astype(F32), 0.0)
    live = jnp.sum(live, axis=1, keepdims=True)
    lane = lax.broadcasted_iota(jnp.int32, (16, 128), 1)
    spot = lax.broadcasted_iota(jnp.int32, (16, 128), 0)
    live = jnp.sum(jnp.where(lane % 16 == spot, live, 0.0), axis=0, keepdims=True)
    lane = lax.broadcasted_iota(jnp.int32, (256, 128), 1)
    block_at = lax.broadcasted_iota(jnp.int32, (256, 128), 0) // BLOCK_LEN
    token = (lane // 16 * 2 + lane % 2).astype(F32)
    usable = (block_at == lane % 16 // 4) & (token < live)
    for head in range(8):
        part = slice(head * HD, (head + 1) * HD)
        scores = lax.dot_general(
            queries_ref[:, part], keys[:, part], (((1,), (1,)), ((), ())),
            preferred_element_type=F32,
        )
        scores = jnp.where(usable, scores * HD ** (-0.5), -1e30)
        powers = jnp.exp(scores - jnp.max(scores, axis=-1, keepdims=True))
        weights = (powers / jnp.sum(powers, axis=-1, keepdims=True)).astype(BF16)
        attended_ref[:, part] = jnp.dot(
            weights, values[:, part], preferred_element_type=F32
        ).astype(BF16)

    wait(ff.at[:, pl.ds(0, 60)], ff_sent)

    @pl.when(whole)
    def _():
        wait(ff.at[:, pl.ds(0, 4)], far_sent)

    @pl.when(jnp.logical_not(whole))
    def _():
        wait(ff.at[:, pl.ds(0, 2)], far_sent)

    wait(kv.at[0, :, pl.ds(0, 63)], kv_sent)
    wait(kv.at[pl.ds(0, 3)], y_sent)

    @pl.when(holder)
    def _():
        wait(held.at[pl.ds(0, 31)], first_sent)
        wait(held.at[pl.ds(0, 63)], second_sent)

    @pl.when(jnp.logical_not(holder))
    def _():
        wait(held.at[pl.ds(0, 32)], first_sent)

    wait(arrived.at[pl.ds(0, 4)], core_sent.at[0])
    for n in range(4):
        wait(mixed.at[n], core_sent.at[n + 1])


def local(
    neighbour_rows,
    lengths,
    block_rows,
    queries,
    encoder_gain,
    weight_in,
    weight_out,
    weight_key,
    weight_value,
):
    dma = pltpu.SemaphoreType.DMA
    vmem = pl.BlockSpec(memory_space=pltpu.VMEM)
    return pl.pallas_call(
        kernel,
        out_shape=jax.ShapeDtypeStruct(queries.shape, BF16),
        in_specs=[pl.BlockSpec(memory_space=pl.ANY)] * 9,
        out_specs=vmem,
        scratch_shapes=[
            pltpu.VMEM((2, NW, 16, 896), BF16),
            pltpu.VMEM((4, 2, NW, 16, 256), BF16),
            pltpu.VMEM((8, 128, 128), BF16),
            pltpu.VMEM((NW, 16, 128), BF16),
            pltpu.VMEM((NW, 16, 128), BF16),
            pltpu.VMEM((8, 128, 128), BF16),
            pltpu.VMEM((4, 128, 256), F32),
            pltpu.VMEM((4, 128, 256), F32),
            pltpu.VMEM((NW * 16, 1), F32),
            pltpu.VMEM((1, NW * 16), F32),
            pltpu.VMEM((128, 1024), BF16),
            pltpu.VMEM((128, 1024), BF16),
            pltpu.VMEM((128, 896), BF16),
            pltpu.VMEM((1, 512), jnp.int32),
            pltpu.VMEM((2, 256), jnp.int32),
            pltpu.VMEM((256, 1024), BF16),
            pltpu.VMEM((896,), F32),
            pltpu.VMEM((14, 896), BF16),
            pltpu.VMEM((14, 896), BF16),
            pltpu.VMEM((14, 1024), BF16),
            pltpu.VMEM((14, 1024), BF16),
        ]
        + [dma((4,))] * 10
        + [dma] * 7
        + [dma((5,))] * 2
        + [dma((9,)), dma, dma],
        compiler_params=pltpu.CompilerParams(
            collective_id=0, has_side_effects=True, vmem_limit_bytes=60 * 2**20
        ),
        name="route_encode_attend",
    )(
        neighbour_rows.reshape(-1, neighbour_rows.shape[-1]),
        lengths.reshape(1, -1),
        block_rows.T,
        queries,
        encoder_gain,
        weight_in,
        weight_out.T,
        weight_key,
        weight_value,
    )


def solution(mesh):
    in_specs = (
        P(("dp", "wide"), None, None),
        P("dp"),
        P("dp", None),
        P(("dp", "wide"), "mp"),
        P(),
        P("wide", "mp"),
        P("mp", "wide"),
        P("wide", "mp"),
        P("wide", "mp"),
    )
    out_specs = P(("dp", "wide"), "mp")
    return jax.shard_map(local, mesh=mesh, in_specs=in_specs, out_specs=out_specs, check_vma=False)
```

```python
import jax
import jax.numpy as jnp
from jax import lax
from jax.experimental import pallas as pl
from jax.experimental.pallas import tpu as pltpu
from jax.sharding import PartitionSpec as P

HD = 128
BLOCK_LEN = 64
NEIGHBOURS = 2
NY, NZ, NX = 4, 16, 4
NW = NZ * NX
MESH = pl.DeviceIdType.MESH
BF16 = jnp.bfloat16
F32 = jnp.float32
WAVES = (0, -4, 4, 8)


def one_hot(mask):
    return mask.astype(F32).astype(BF16)


def kernel(
    rows_hbm, lengths_hbm, blocks_hbm, queries_hbm, gain_hbm,
    in_hbm, out_hbm, key_hbm, value_hbm, attended_ref,
    ff, kv, tiles, held, sorted_rows, arrived, mixed, other, index, gain, keys, values,
    picks,
    rows_ref, lengths_ref, blocks_ref, queries_ref, gain_ref, in_ref, out_ref, key_ref, value_ref,
    ff_z1, ff_z2, ff_x, ff_xf, kv_z1, kv_z2, kv_x, kv_xf, kv_y, kv_yf,
    ff_sent, kv_sent, y_sent, first_sent, first_recv, second_sent, second_recv,
    core_sent, core_recv, loaded, far_sent, far_recv,
):
    y = lax.axis_index("dp")
    me = lax.axis_index("wide")
    core = lax.axis_index("mp")
    z = me // NX
    x = me % NX
    holder = me % 2 == core
    side = 2 - 4 * core
    spans = (0, -1, 1, -side)

    def slot(zz, xx):
        return ((zz + 2 * NZ) % NZ) * NX + (xx + 2 * NX) % NX

    def plane(yy):
        return (yy + NY) % NY

    loads = [
        pltpu.make_async_copy(src, dst, loaded.at[n])
        for n, (src, dst) in enumerate(
            (
                (in_hbm, in_ref), (out_hbm, out_ref), (key_hbm, key_ref), (value_hbm, value_ref),
                (rows_hbm, rows_ref), (gain_hbm, gain_ref), (blocks_hbm, blocks_ref),
                (lengths_hbm, lengths_ref), (queries_hbm, queries_ref),
            )
        )
    ]
    for load in loads:
        load.start()
    barrier = pltpu.get_barrier_semaphore()

    def greet(step, carry):
        for far in (NW // 2 + step, NW // 2 - step):
            pl.semaphore_signal(
                barrier, inc=1, device_id=(y, (me + far) % NW, core), device_id_type=MESH
            )
        return carry

    pl.semaphore_signal(
        barrier, inc=1, device_id=(y, (me + NW // 2) % NW, core), device_id_type=MESH
    )
    lax.fori_loop(1, NW // 2, greet, 0)
    for target in (
        (plane(y + 1), me, core), (plane(y - 1), me, core), (plane(y + 2), me, core),
        (y, me, 1 - core),
    ):
        pl.semaphore_signal(barrier, inc=1, device_id=target, device_id_type=MESH)

    for load in loads[:4]:
        load.wait()
    row = lax.broadcasted_iota(jnp.int32, (16, 14), 0)
    pad = one_hot(row == lax.broadcasted_iota(jnp.int32, (16, 14), 1))

    def padded(shard):
        return jnp.dot(pad, shard, preferred_element_type=F32).astype(BF16)

    ff[0, pl.ds(me, 1)] = padded(in_ref[...])[None]
    ff[1, pl.ds(me, 1)] = padded(out_ref[...])[None]
    for n, ref in ((0, key_ref), (1, value_ref)):
        shard = padded(ref[:, pl.ds(pl.multiple_of(y * 256, 256), 256)])
        kv[pl.ds(y, 1), n, pl.ds(me, 1)] = shard[None, None]

    pl.semaphore_wait(barrier, NW + 3)

    def prepare():
        for load in loads[4:8]:
            load.wait()
        at = lax.broadcasted_iota(jnp.int32, (128, 128), 0)
        of = lax.broadcasted_iota(jnp.int32, (128, 128), 1)
        pairs = one_hot(of == (at % 16) // 2 * 16 + at // 16 * 2 + at % 2)
        in_pairs = jnp.dot(pairs, rows_ref[...], preferred_element_type=F32).astype(BF16)
        feature = lax.broadcasted_iota(jnp.int32, (896, 128), 0)
        lane = lax.broadcasted_iota(jnp.int32, (1, 128), 1)
        exact = gain_ref[...].reshape(1, 896)
        high = exact.astype(BF16).astype(F32)
        middle = (exact - high).astype(BF16).astype(F32)
        low = exact - high - middle
        term = lax.broadcasted_iota(jnp.int32, (16, 896), 0)
        terms = jnp.where(
            term == 0, high, jnp.where(term == 1, middle, jnp.where(term == 2, low, 0.0))
        ).astype(BF16)
        for tile in range(8):
            wanted = jnp.where(
                lane % 16 < 14, (tile * 8 + lane // 16) * 14 + lane % 16, -1
            )
            pick = one_hot(feature == wanted)
            tiles[tile] = jnp.dot(in_pairs, pick, preferred_element_type=F32).astype(BF16)
            gain[:, tile * 128 : (tile + 1) * 128] = jnp.sum(
                jnp.dot(terms, pick, preferred_element_type=F32), axis=0, keepdims=True
            )

    def number():
        listed = blocks_ref[...]
        block = lax.broadcasted_iota(jnp.int32, (NW * 16, 256), 1)
        place = lax.broadcasted_iota(jnp.int32, (NW * 16, 256), 0)
        spread = one_hot(block == place // 4)
        halves = []
        for value in (listed // 2, listed % 2):
            value = jnp.broadcast_to(value[:, None], (NEIGHBOURS, 8, 256)).reshape(16, 256)
            halves.append(
                lax.dot_general(
                    spread, value.astype(F32).astype(BF16), (((1,), (1,)), ((), ())),
                    preferred_element_type=F32,
                )
            )
        both = 4.0 * halves[0] + 2.0 * halves[1]
        place = lax.broadcasted_iota(jnp.int32, (NW * 16, 1), 0)
        half = (place % 2).astype(F32)
        index[...] = jnp.where(place // 2 % 2 == 0, both[:, 0:1], both[:, 8:9]) + half

    def send(src, dst, send_sem, recv_sem, target):
        pltpu.make_async_remote_copy(
            src_ref=src, dst_ref=dst, send_sem=send_sem, recv_sem=recv_sem,
            device_id=target, device_id_type=MESH,
        ).start()

    def wait(ref, sem):
        pltpu.make_async_copy(ref, ref, sem).wait()

    def first(step, carry):
        apart = NW // 4 + (step + 1) // 2 * (1 - 2 * (step % 2))
        spot = (me // 2 + apart) % (NW // 2)
        target = spot * 2 + core
        src = tiles.at[core * 4 + spot % 4, pl.ds(pl.multiple_of(spot // 4 * 16, 16), 16)]

        @pl.when(target == me)
        def _():
            pltpu.make_async_copy(src, held.at[me], first_recv).start()

        @pl.when(target != me)
        def _():
            send(src, held.at[me], first_sent, first_recv, (y, target, core))

        return carry

    def route():
        lax.fori_loop(0, NW // 2, first, 0)


    class Ff:
        z1, z2, xs, xf, sent = ff_z1, ff_z2, ff_x, ff_xf, ff_sent

        @staticmethod
        def at(place, count=1):
            return ff.at[:, pl.ds(place, count)]

    class Kv:
        z1, z2, xs, xf, sent = kv_z1, kv_z2, kv_x, kv_xf, kv_sent

        @staticmethod
        def at(place, count=1):
            return kv.at[y, :, pl.ds(place, count)]

    def move(part, place, sem, target):
        send(part.at(place), part.at(place), part.sent, sem, target)

    def z1_send(wave):
        off = (4, -4, 8)[wave - 1]
        move(Kv, me, kv_z1.at[wave], (y, slot(z + off, x), core))

    turn = (y + core) % 2
    whole = y < 2
    fetched = ff_z1.at[1 + turn]

    def fetch():
        @pl.when(whole)
        def _():
            ref = ff.at[:, pl.ds(me, 1)]
            send(ref, ref, far_sent, fetched, (y, slot(z + 4 - 8 * turn, x), core))

        @pl.when(jnp.logical_not(whole))
        def _():
            ref = ff.at[y % 2, pl.ds(me, 1)]
            send(ref, ref, far_sent, far_recv, (y, slot(z + 8, x), core))

    def spread():
        @pl.when(whole)
        def _():
            wait(ff.at[:, pl.ds(0, 1)], fetched)
            ref = ff.at[:, pl.ds(slot(z - 4 + 8 * turn, x), 1)]
            for off in (1, -1, 2):
                send(ref, ref, far_sent, fetched, (plane(y + off), me, core))

        @pl.when(jnp.logical_not(whole))
        def _():
            wait(ff.at[0, pl.ds(0, 1)], far_recv)
            ref = ff.at[y % 2, pl.ds(slot(z + 8, x), 1)]
            for off in (1, -1, 2):
                send(ref, ref, far_sent, ff_z1.at[3], (plane(y + off), me, core))

    def z2_send(part, wave):
        if part is Kv and wave:
            wait(part.at(0), part.z1.at[wave])
        elif wave == 3:

            @pl.when(whole)
            def _():
                wait(ff.at[:, pl.ds(0, 1)], ff_z1.at[3])

            @pl.when(jnp.logical_not(whole))
            def _():
                wait(ff.at[0, pl.ds(0, 1)], ff_z1.at[3])
        elif wave:

            @pl.when(jnp.logical_not(whole & (turn == wave - 1)))
            def _():
                wait(ff.at[:, pl.ds(0, 1)], ff_z1.at[wave])

        for off in (1, -1, side):
            move(part, slot(z + WAVES[wave], x), part.z2.at[wave], (y, slot(z + off, x), core))

    def own_send(part, wave):
        for off in (1, -1):
            move(part, slot(z + WAVES[wave], x), part.xs.at[wave], (y, slot(z, x + off), core))

    def x_send(part, wave):
        wait(part.at(0, 3), part.z2.at[wave])
        for span in spans[1:]:
            for off in (1, -1):
                move(
                    part, slot(z + WAVES[wave] + span, x), part.xs.at[wave],
                    (y, slot(z, x + off), core),
                )

    def xf_send(part, wave):
        wait(part.at(0, 8), part.xs.at[wave])
        for n, span in enumerate(spans):
            off = 1 if n < 2 else -1
            move(
                part, slot(z + WAVES[wave] + span, x - off), part.xf.at[wave],
                (y, slot(z, x + off), core),
            )

    def x_done(part, wave):
        wait(part.at(0, 4), part.xf.at[wave])

    def block(part_y, zz):
        return kv.at[part_y, :, pl.ds(slot(zz, 0), NX)]

    def y_send(wave):
        x_done(Kv, wave)
        for span in spans:
            for off in (1, -1):
                ref = block(y, z + WAVES[wave] + span)
                send(ref, ref, y_sent, kv_y.at[wave], (plane(y + off), me, core))

    def yf_send(wave):
        wait(kv.at[0, :, pl.ds(0, 32)], kv_y.at[wave])
        for n, span in enumerate(spans):
            off = 1 if n < 2 else -1
            ref = block(plane(y - off), z + WAVES[wave] + span)
            send(ref, ref, y_sent, kv_yf.at[wave], (plane(y + off), me, core))

    def y_done(wave):
        wait(kv.at[0, :, pl.ds(0, 16)], kv_yf.at[wave])

    def mark():
        number()

        @pl.when(holder)
        def _():
            source = lax.broadcasted_iota(jnp.int32, (256, NW * 16), 1).astype(F32)

            def part(step, carry):
                start = pl.multiple_of(step * 256, 256)
                picks[pl.ds(start, 256)] = one_hot(index[pl.ds(start, 256)] == source)
                return carry

            lax.fori_loop(0, 4, part, 0)

    def permute():
        @pl.when(holder)
        def _():
            wait(held, first_recv)
            rows = held[...].reshape(NW * 16, 128)

            def part(step, carry):
                start = pl.multiple_of(step * 256, 256)
                pick = picks[pl.ds(start, 256)]
                moved = jnp.dot(pick, rows, preferred_element_type=F32).astype(BF16)
                sorted_rows[pl.ds(step * 16, 16)] = moved.reshape(16, 16, 128)
                return carry

            lax.fori_loop(0, 4, part, 0)
            spot = me // 2
            dst = arrived.at[core * 4 + spot % 4, pl.ds(pl.multiple_of(spot // 4 * 16, 16), 16)]

            def second(step, carry):
                apart = NW // 2 + step // 2 * (1 - 2 * (step % 2))
                target = (me + apart) % NW
                send(sorted_rows.at[target], dst, second_sent, second_recv, (y, target, core))
                return carry

            pltpu.make_async_copy(sorted_rows.at[me], dst, second_recv).start()
            lax.fori_loop(1, NW, second, 0)

    def swap_cores():
        wait(arrived.at[pl.ds(0, 4)], second_recv)
        half = arrived.at[pl.ds(core * 4, 4)]
        send(half, half, core_sent.at[0], core_recv.at[0], (y, me, 1 - core))

    z2_send(Kv, 0)
    z1_send(1)
    z1_send(2)
    z2_send(Ff, 0)
    own_send(Ff, 0)
    own_send(Kv, 0)
    fetch()
    x_send(Kv, 0)
    prepare()
    z1_send(3)
    z2_send(Kv, 2)
    own_send(Kv, 2)
    x_send(Ff, 0)
    z2_send(Kv, 1)
    xf_send(Kv, 0)
    route()
    own_send(Kv, 1)
    x_send(Kv, 2)
    mark()
    spread()
    xf_send(Ff, 0)
    z2_send(Kv, 3)
    y_send(0)
    x_send(Kv, 1)
    own_send(Kv, 3)
    xf_send(Kv, 2)
    z2_send(Ff, 1)
    x_send(Kv, 3)
    z2_send(Ff, 3)
    own_send(Ff, 3)
    xf_send(Kv, 1)
    own_send(Ff, 1)
    z2_send(Ff, 2)
    y_send(2)
    xf_send(Kv, 3)
    own_send(Ff, 2)
    x_send(Ff, 1)
    y_send(1)
    x_send(Ff, 3)
    permute()
    x_send(Ff, 2)
    y_send(3)
    yf_send(2)
    xf_send(Ff, 3)
    yf_send(0)
    xf_send(Ff, 1)
    yf_send(3)
    xf_send(Ff, 2)
    yf_send(1)
    swap_cores()

    wait(arrived.at[pl.ds(0, 4)], core_recv.at[0])
    inputs = jnp.concatenate([arrived[tile] for tile in range(8)], axis=1).astype(F32)
    squares = jnp.sum(inputs * inputs, axis=-1, keepdims=True) * (1.0 / 896)
    normed = (inputs * lax.rsqrt(squares + 1e-06) * gain[...]).astype(BF16)
    for wave in range(4):
        x_done(Ff, wave)
    hidden = []
    for start, size in ((0, 256), (256, 256), (512, 256), (768, 128)):
        weight = ff[0, :, :, start : start + size].reshape(NW * 16, size)
        preact = jnp.dot(normed, weight, preferred_element_type=F32)
        hidden.append(jax.nn.gelu(preact).astype(BF16))
    hidden = jnp.concatenate(hidden, axis=1)
    for n in range(4):
        weight = ff[1, n * 16 : (n + 1) * 16].reshape(256, 896)
        mixed[n] = lax.dot_general(
            hidden, weight, (((1,), (1,)), ((), ())), preferred_element_type=F32
        )
        send(mixed.at[n], other.at[n], core_sent.at[n + 1], core_recv.at[n + 1], (y, me, 1 - core))
    encoded = []
    for n in range(4):
        wait(other.at[n], core_recv.at[n + 1])
        part = inputs[:, n * 256 : (n + 1) * 256] + (mixed[n] + other[n])
        encoded.append(part.astype(BF16))
    encoded = jnp.concatenate(encoded, axis=1)
    for wave in range(4):
        y_done(wave)
    for q in range(4):
        for n, out in ((0, keys), (1, values)):
            weight = kv[q, n].reshape(NW * 16, 256)
            out[:, q * 256 : (q + 1) * 256] = jnp.dot(
                encoded, weight, preferred_element_type=F32
            ).astype(BF16)

    loads[8].wait()
    mine = index[pl.ds(pl.multiple_of(me * 16, 16), 16)]
    source = lax.broadcasted_iota(jnp.int32, (16, 512), 1).astype(F32) * 2.0
    hit = (mine == source) | (mine == source + 1.0)
    live = jnp.where(hit, lengths_ref[...].astype(F32), 0.0)
    live = jnp.sum(live, axis=1, keepdims=True)
    lane = lax.broadcasted_iota(jnp.int32, (16, 128), 1)
    spot = lax.broadcasted_iota(jnp.int32, (16, 128), 0)
    live = jnp.sum(jnp.where(lane % 16 == spot, live, 0.0), axis=0, keepdims=True)
    lane = lax.broadcasted_iota(jnp.int32, (256, 128), 1)
    block_at = lax.broadcasted_iota(jnp.int32, (256, 128), 0) // BLOCK_LEN
    token = (lane // 16 * 2 + lane % 2).astype(F32)
    usable = (block_at == lane % 16 // 4) & (token < live)
    for head in range(8):
        part = slice(head * HD, (head + 1) * HD)
        scores = lax.dot_general(
            queries_ref[:, part], keys[:, part], (((1,), (1,)), ((), ())),
            preferred_element_type=F32,
        )
        scores = jnp.where(usable, scores * HD ** (-0.5), -1e30)
        powers = jnp.exp(scores - jnp.max(scores, axis=-1, keepdims=True))
        weights = (powers / jnp.sum(powers, axis=-1, keepdims=True)).astype(BF16)
        attended_ref[:, part] = jnp.dot(
            weights, values[:, part], preferred_element_type=F32
        ).astype(BF16)

    wait(ff.at[:, pl.ds(0, 60)], ff_sent)

    @pl.when(whole)
    def _():
        wait(ff.at[:, pl.ds(0, 4)], far_sent)

    @pl.when(jnp.logical_not(whole))
    def _():
        wait(ff.at[:, pl.ds(0, 2)], far_sent)

    wait(kv.at[0, :, pl.ds(0, 63)], kv_sent)
    wait(kv.at[pl.ds(0, 3)], y_sent)

    @pl.when(holder)
    def _():
        wait(held.at[pl.ds(0, 31)], first_sent)
        wait(held.at[pl.ds(0, 63)], second_sent)

    @pl.when(jnp.logical_not(holder))
    def _():
        wait(held.at[pl.ds(0, 32)], first_sent)

    wait(arrived.at[pl.ds(0, 4)], core_sent.at[0])
    for n in range(4):
        wait(mixed.at[n], core_sent.at[n + 1])


def local(
    neighbour_rows,
    lengths,
    block_rows,
    queries,
    encoder_gain,
    weight_in,
    weight_out,
    weight_key,
    weight_value,
):
    dma = pltpu.SemaphoreType.DMA
    vmem = pl.BlockSpec(memory_space=pltpu.VMEM)
    return pl.pallas_call(
        kernel,
        out_shape=jax.ShapeDtypeStruct(queries.shape, BF16),
        in_specs=[pl.BlockSpec(memory_space=pl.ANY)] * 9,
        out_specs=vmem,
        scratch_shapes=[
            pltpu.VMEM((2, NW, 16, 896), BF16),
            pltpu.VMEM((4, 2, NW, 16, 256), BF16),
            pltpu.VMEM((8, 128, 128), BF16),
            pltpu.VMEM((NW, 16, 128), BF16),
            pltpu.VMEM((NW, 16, 128), BF16),
            pltpu.VMEM((8, 128, 128), BF16),
            pltpu.VMEM((4, 128, 256), F32),
            pltpu.VMEM((4, 128, 256), F32),
            pltpu.VMEM((NW * 16, 1), F32),
            pltpu.VMEM((1, NW * 16), F32),
            pltpu.VMEM((128, 1024), BF16),
            pltpu.VMEM((128, 1024), BF16),
            pltpu.VMEM((NW * 16, NW * 16), BF16),
            pltpu.VMEM((128, 896), BF16),
            pltpu.VMEM((1, 512), jnp.int32),
            pltpu.VMEM((2, 256), jnp.int32),
            pltpu.VMEM((256, 1024), BF16),
            pltpu.VMEM((896,), F32),
            pltpu.VMEM((14, 896), BF16),
            pltpu.VMEM((14, 896), BF16),
            pltpu.VMEM((14, 1024), BF16),
            pltpu.VMEM((14, 1024), BF16),
        ]
        + [dma((4,))] * 10
        + [dma] * 7
        + [dma((5,))] * 2
        + [dma((9,)), dma, dma],
        compiler_params=pltpu.CompilerParams(
            collective_id=0, has_side_effects=True, vmem_limit_bytes=60 * 2**20
        ),
        name="route_encode_attend",
    )(
        neighbour_rows.reshape(-1, neighbour_rows.shape[-1]),
        lengths.reshape(1, -1),
        block_rows.T,
        queries,
        encoder_gain,
        weight_in,
        weight_out.T,
        weight_key,
        weight_value,
    )


def solution(mesh):
    in_specs = (
        P(("dp", "wide"), None, None),
        P("dp"),
        P("dp", None),
        P(("dp", "wide"), "mp"),
        P(),
        P("wide", "mp"),
        P("mp", "wide"),
        P("wide", "mp"),
        P("wide", "mp"),
    )
    out_specs = P(("dp", "wide"), "mp")
    return jax.shard_map(local, mesh=mesh, in_specs=in_specs, out_specs=out_specs, check_vma=False)
```

```python
import jax
import jax.numpy as jnp
from jax import lax
from jax.experimental import pallas as pl
from jax.experimental.pallas import tpu as pltpu
from jax.sharding import PartitionSpec as P

HD = 128
BLOCK_LEN = 64
NEIGHBOURS = 2
NY, NZ, NX = 4, 16, 4
NW = NZ * NX
MESH = pl.DeviceIdType.MESH
BF16 = jnp.bfloat16
F32 = jnp.float32
WAVES = (0, -4, 4, 8)


def one_hot(mask):
    return mask.astype(F32).astype(BF16)


def kernel(
    rows_hbm, lengths_hbm, blocks_hbm, queries_hbm, gain_hbm,
    in_hbm, out_hbm, key_hbm, value_hbm, attended_ref,
    ff, kv, tiles, held, sorted_rows, arrived, mixed, other, index, gain, keys, values,
    picks,
    rows_ref, lengths_ref, blocks_ref, queries_ref, gain_ref, in_ref, out_ref, key_ref, value_ref,
    ff_z1, ff_z2, ff_x, ff_xf, kv_z1, kv_z2, kv_x, kv_xf, kv_y, kv_yf,
    ff_sent, kv_sent, y_sent, first_sent, first_recv, second_sent, second_recv,
    core_sent, core_recv, loaded, far_sent, far_recv,
):
    y = lax.axis_index("dp")
    me = lax.axis_index("wide")
    core = lax.axis_index("mp")
    z = me // NX
    x = me % NX
    holder = me % 2 == core
    side = 2 - 4 * core
    spans = (0, -1, 1, -side)

    def slot(zz, xx):
        return ((zz + 2 * NZ) % NZ) * NX + (xx + 2 * NX) % NX

    def plane(yy):
        return (yy + NY) % NY

    loads = [
        pltpu.make_async_copy(src, dst, loaded.at[n])
        for n, (src, dst) in enumerate(
            (
                (in_hbm, in_ref), (out_hbm, out_ref), (key_hbm, key_ref), (value_hbm, value_ref),
                (rows_hbm, rows_ref), (gain_hbm, gain_ref), (blocks_hbm, blocks_ref),
                (lengths_hbm, lengths_ref), (queries_hbm, queries_ref),
            )
        )
    ]
    for load in loads:
        load.start()
    barrier = pltpu.get_barrier_semaphore()

    def greet(step, carry):
        for far in (NW // 2 + step, NW // 2 - step):
            pl.semaphore_signal(
                barrier, inc=1, device_id=(y, (me + far) % NW, core), device_id_type=MESH
            )
        return carry

    pl.semaphore_signal(
        barrier, inc=1, device_id=(y, (me + NW // 2) % NW, core), device_id_type=MESH
    )
    lax.fori_loop(1, NW // 2, greet, 0)
    for target in (
        (plane(y + 1), me, core), (plane(y - 1), me, core), (plane(y + 2), me, core),
        (y, me, 1 - core),
    ):
        pl.semaphore_signal(barrier, inc=1, device_id=target, device_id_type=MESH)

    for load in loads[:4]:
        load.wait()
    row = lax.broadcasted_iota(jnp.int32, (16, 14), 0)
    pad = one_hot(row == lax.broadcasted_iota(jnp.int32, (16, 14), 1))

    def padded(shard):
        return jnp.dot(pad, shard, preferred_element_type=F32).astype(BF16)

    ff[0, pl.ds(me, 1)] = padded(in_ref[...])[None]
    ff[1, pl.ds(me, 1)] = padded(out_ref[...])[None]
    for n, ref in ((0, key_ref), (1, value_ref)):
        shard = padded(ref[:, pl.ds(pl.multiple_of(y * 256, 256), 256)])
        kv[pl.ds(y, 1), n, pl.ds(me, 1)] = shard[None, None]

    pl.semaphore_wait(barrier, NW + 3)

    def prepare():
        for load in loads[4:8]:
            load.wait()
        at = lax.broadcasted_iota(jnp.int32, (128, 128), 0)
        of = lax.broadcasted_iota(jnp.int32, (128, 128), 1)
        pairs = one_hot(of == (at % 16) // 2 * 16 + at // 16 * 2 + at % 2)
        in_pairs = jnp.dot(pairs, rows_ref[...], preferred_element_type=F32).astype(BF16)
        feature = lax.broadcasted_iota(jnp.int32, (896, 128), 0)
        lane = lax.broadcasted_iota(jnp.int32, (1, 128), 1)
        exact = gain_ref[...].reshape(1, 896)
        high = exact.astype(BF16).astype(F32)
        middle = (exact - high).astype(BF16).astype(F32)
        low = exact - high - middle
        term = lax.broadcasted_iota(jnp.int32, (16, 896), 0)
        terms = jnp.where(
            term == 0, high, jnp.where(term == 1, middle, jnp.where(term == 2, low, 0.0))
        ).astype(BF16)
        for tile in range(8):
            wanted = jnp.where(
                lane % 16 < 14, (tile * 8 + lane // 16) * 14 + lane % 16, -1
            )
            pick = one_hot(feature == wanted)
            tiles[tile] = jnp.dot(in_pairs, pick, preferred_element_type=F32).astype(BF16)
            gain[:, tile * 128 : (tile + 1) * 128] = jnp.sum(
                jnp.dot(terms, pick, preferred_element_type=F32), axis=0, keepdims=True
            )

    def number():
        listed = blocks_ref[...]
        block = lax.broadcasted_iota(jnp.int32, (NW * 16, 256), 1)
        place = lax.broadcasted_iota(jnp.int32, (NW * 16, 256), 0)
        spread = one_hot(block == place // 4)
        halves = []
        for value in (listed // 2, listed % 2):
            value = jnp.broadcast_to(value[:, None], (NEIGHBOURS, 8, 256)).reshape(16, 256)
            halves.append(
                lax.dot_general(
                    spread, value.astype(F32).astype(BF16), (((1,), (1,)), ((), ())),
                    preferred_element_type=F32,
                )
            )
        both = 4.0 * halves[0] + 2.0 * halves[1]
        place = lax.broadcasted_iota(jnp.int32, (NW * 16, 1), 0)
        half = (place % 2).astype(F32)
        index[...] = jnp.where(place // 2 % 2 == 0, both[:, 0:1], both[:, 8:9]) + half

    def send(src, dst, send_sem, recv_sem, target):
        pltpu.make_async_remote_copy(
            src_ref=src, dst_ref=dst, send_sem=send_sem, recv_sem=recv_sem,
            device_id=target, device_id_type=MESH,
        ).start()

    def wait(ref, sem):
        pltpu.make_async_copy(ref, ref, sem).wait()

    def first(step, carry):
        apart = NW // 4 + (step + 1) // 2 * (1 - 2 * (step % 2))
        spot = (me // 2 + apart) % (NW // 2)
        target = spot * 2 + core
        src = tiles.at[core * 4 + spot % 4, pl.ds(pl.multiple_of(spot // 4 * 16, 16), 16)]

        @pl.when(target == me)
        def _():
            pltpu.make_async_copy(src, held.at[me], first_recv).start()

        @pl.when(target != me)
        def _():
            send(src, held.at[me], first_sent, first_recv, (y, target, core))

        return carry

    def route():
        lax.fori_loop(0, NW // 2, first, 0)


    class Ff:
        z1, z2, xs, xf, sent = ff_z1, ff_z2, ff_x, ff_xf, ff_sent

        @staticmethod
        def at(place, count=1):
            return ff.at[:, pl.ds(place, count)]

    class Kv:
        z1, z2, xs, xf, sent = kv_z1, kv_z2, kv_x, kv_xf, kv_sent

        @staticmethod
        def at(place, count=1):
            return kv.at[y, :, pl.ds(place, count)]

    def move(part, place, sem, target):
        send(part.at(place), part.at(place), part.sent, sem, target)

    def z1_send(wave):
        off = (4, -4, 8)[wave - 1]
        move(Kv, me, kv_z1.at[wave], (y, slot(z + off, x), core))

    turn = (y + core) % 2
    whole = y < 2
    fetched = ff_z1.at[1 + turn]

    def fetch():
        @pl.when(whole)
        def _():
            ref = ff.at[:, pl.ds(me, 1)]
            send(ref, ref, far_sent, fetched, (y, slot(z + 4 - 8 * turn, x), core))

        @pl.when(jnp.logical_not(whole))
        def _():
            ref = ff.at[y % 2, pl.ds(me, 1)]
            send(ref, ref, far_sent, far_recv, (y, slot(z + 8, x), core))

    def spread():
        @pl.when(whole)
        def _():
            wait(ff.at[:, pl.ds(0, 1)], fetched)
            ref = ff.at[:, pl.ds(slot(z - 4 + 8 * turn, x), 1)]
            for off in (1, -1, 2):
                send(ref, ref, far_sent, fetched, (plane(y + off), me, core))

        @pl.when(jnp.logical_not(whole))
        def _():
            wait(ff.at[0, pl.ds(0, 1)], far_recv)
            ref = ff.at[y % 2, pl.ds(slot(z + 8, x), 1)]
            for off in (1, -1, 2):
                send(ref, ref, far_sent, ff_z1.at[3], (plane(y + off), me, core))

    def z2_send(part, wave):
        if part is Kv and wave:
            wait(part.at(0), part.z1.at[wave])
        elif wave == 3:

            @pl.when(whole)
            def _():
                wait(ff.at[:, pl.ds(0, 1)], ff_z1.at[3])

            @pl.when(jnp.logical_not(whole))
            def _():
                wait(ff.at[0, pl.ds(0, 1)], ff_z1.at[3])
        elif wave:

            @pl.when(jnp.logical_not(whole & (turn == wave - 1)))
            def _():
                wait(ff.at[:, pl.ds(0, 1)], ff_z1.at[wave])

        for off in (1, -1, side):
            move(part, slot(z + WAVES[wave], x), part.z2.at[wave], (y, slot(z + off, x), core))

    def own_send(part, wave):
        for off in (1, -1):
            move(part, slot(z + WAVES[wave], x), part.xs.at[wave], (y, slot(z, x + off), core))

    def x_send(part, wave):
        wait(part.at(0, 3), part.z2.at[wave])
        for span in spans[1:]:
            for off in (1, -1):
                move(
                    part, slot(z + WAVES[wave] + span, x), part.xs.at[wave],
                    (y, slot(z, x + off), core),
                )

    def xf_send(part, wave):
        wait(part.at(0, 8), part.xs.at[wave])
        for n, span in enumerate(spans):
            off = 1 if n < 2 else -1
            move(
                part, slot(z + WAVES[wave] + span, x - off), part.xf.at[wave],
                (y, slot(z, x + off), core),
            )

    def x_done(part, wave):
        wait(part.at(0, 4), part.xf.at[wave])

    def block(part_y, zz):
        return kv.at[part_y, :, pl.ds(slot(zz, 0), NX)]

    def y_send(wave):
        x_done(Kv, wave)
        for span in spans:
            for off in (1, -1):
                ref = block(y, z + WAVES[wave] + span)
                send(ref, ref, y_sent, kv_y.at[wave], (plane(y + off), me, core))

    def yf_send(wave):
        wait(kv.at[0, :, pl.ds(0, 32)], kv_y.at[wave])
        for n, span in enumerate(spans):
            off = 1 if n < 2 else -1
            ref = block(plane(y - off), z + WAVES[wave] + span)
            send(ref, ref, y_sent, kv_yf.at[wave], (plane(y + off), me, core))

    def y_done(wave):
        wait(kv.at[0, :, pl.ds(0, 16)], kv_yf.at[wave])

    def mark():
        number()

        @pl.when(holder)
        def _():
            source = lax.broadcasted_iota(jnp.int32, (256, NW * 16), 1).astype(F32)

            def part(step, carry):
                start = pl.multiple_of(step * 256, 256)
                picks[pl.ds(start, 256)] = one_hot(index[pl.ds(start, 256)] == source)
                return carry

            lax.fori_loop(0, 4, part, 0)

    def permute():
        @pl.when(holder)
        def _():
            wait(held, first_recv)
            rows = held[...].reshape(NW * 16, 128)

            def part(step, carry):
                start = pl.multiple_of(step * 256, 256)
                pick = picks[pl.ds(start, 256)]
                moved = jnp.dot(pick, rows, preferred_element_type=F32).astype(BF16)
                sorted_rows[pl.ds(step * 16, 16)] = moved.reshape(16, 16, 128)
                return carry

            lax.fori_loop(0, 4, part, 0)
            spot = me // 2
            dst = arrived.at[core * 4 + spot % 4, pl.ds(pl.multiple_of(spot // 4 * 16, 16), 16)]

            def second(step, carry):
                apart = NW // 2 + step // 2 * (1 - 2 * (step % 2))
                target = (me + apart) % NW
                send(sorted_rows.at[target], dst, second_sent, second_recv, (y, target, core))
                return carry

            pltpu.make_async_copy(sorted_rows.at[me], dst, second_recv).start()
            lax.fori_loop(1, NW, second, 0)

    def swap_cores():
        wait(arrived.at[pl.ds(0, 4)], second_recv)
        half = arrived.at[pl.ds(core * 4, 4)]
        send(half, half, core_sent.at[0], core_recv.at[0], (y, me, 1 - core))

    z2_send(Kv, 0)
    z1_send(1)
    z1_send(2)
    z2_send(Ff, 0)
    own_send(Ff, 0)
    own_send(Kv, 0)
    fetch()
    x_send(Kv, 0)
    prepare()
    z1_send(3)
    z2_send(Kv, 2)
    own_send(Kv, 2)
    x_send(Ff, 0)
    z2_send(Kv, 1)
    xf_send(Kv, 0)
    route()
    own_send(Kv, 1)
    x_send(Kv, 2)
    mark()
    spread()
    xf_send(Ff, 0)
    z2_send(Kv, 3)
    y_send(0)
    x_send(Kv, 1)
    own_send(Kv, 3)
    xf_send(Kv, 2)
    z2_send(Ff, 1)
    x_send(Kv, 3)
    z2_send(Ff, 3)
    own_send(Ff, 3)
    xf_send(Kv, 1)
    own_send(Ff, 1)
    z2_send(Ff, 2)
    y_send(2)
    xf_send(Kv, 3)
    own_send(Ff, 2)
    x_send(Ff, 1)
    y_send(1)
    x_send(Ff, 3)
    permute()
    x_send(Ff, 2)
    y_send(3)
    yf_send(2)
    xf_send(Ff, 3)
    yf_send(0)
    xf_send(Ff, 1)
    yf_send(3)
    xf_send(Ff, 2)
    yf_send(1)
    swap_cores()

    mine = index[pl.ds(pl.multiple_of(me * 16, 16), 16)]
    source = lax.broadcasted_iota(jnp.int32, (16, 512), 1).astype(F32) * 2.0
    hit = (mine == source) | (mine == source + 1.0)
    live = jnp.where(hit, lengths_ref[...].astype(F32), 0.0)
    live = jnp.sum(live, axis=1, keepdims=True)
    lane = lax.broadcasted_iota(jnp.int32, (16, 128), 1)
    spot = lax.broadcasted_iota(jnp.int32, (16, 128), 0)
    live = jnp.sum(jnp.where(lane % 16 == spot, live, 0.0), axis=0, keepdims=True)
    lane = lax.broadcasted_iota(jnp.int32, (256, 128), 1)
    block_at = lax.broadcasted_iota(jnp.int32, (256, 128), 0) // BLOCK_LEN
    token = (lane // 16 * 2 + lane % 2).astype(F32)
    usable = (block_at == lane % 16 // 4) & (token < live)

    wait(arrived.at[pl.ds(0, 4)], core_recv.at[0])
    inputs = jnp.concatenate([arrived[tile] for tile in range(8)], axis=1).astype(F32)
    squares = jnp.sum(inputs * inputs, axis=-1, keepdims=True) * (1.0 / 896)
    normed = (inputs * lax.rsqrt(squares + 1e-06) * gain[...]).astype(BF16)
    for wave in range(4):
        x_done(Ff, wave)
    hidden = []
    for start, size in ((0, 256), (256, 256), (512, 256), (768, 128)):
        weight = ff[0, :, :, start : start + size].reshape(NW * 16, size)
        preact = jnp.dot(normed, weight, preferred_element_type=F32)
        hidden.append(jax.nn.gelu(preact).astype(BF16))
    hidden = jnp.concatenate(hidden, axis=1)
    for n in range(4):
        weight = ff[1, n * 16 : (n + 1) * 16].reshape(256, 896)
        mixed[n] = lax.dot_general(
            hidden, weight, (((1,), (1,)), ((), ())), preferred_element_type=F32
        )
        send(mixed.at[n], other.at[n], core_sent.at[n + 1], core_recv.at[n + 1], (y, me, 1 - core))
    encoded = []
    for n in range(4):
        wait(other.at[n], core_recv.at[n + 1])
        part = inputs[:, n * 256 : (n + 1) * 256] + (mixed[n] + other[n])
        encoded.append(part.astype(BF16))
    encoded = jnp.concatenate(encoded, axis=1)
    for wave in range(4):
        y_done(wave)
    for q in range(4):
        for n, out in ((0, keys), (1, values)):
            weight = kv[q, n].reshape(NW * 16, 256)
            out[:, q * 256 : (q + 1) * 256] = jnp.dot(
                encoded, weight, preferred_element_type=F32
            ).astype(BF16)

    loads[8].wait()
    for head in range(8):
        part = slice(head * HD, (head + 1) * HD)
        scores = lax.dot_general(
            queries_ref[:, part], keys[:, part], (((1,), (1,)), ((), ())),
            preferred_element_type=F32,
        )
        scores = jnp.where(usable, scores * HD ** (-0.5), -1e30)
        powers = jnp.exp(scores - jnp.max(scores, axis=-1, keepdims=True))
        weights = (powers / jnp.sum(powers, axis=-1, keepdims=True)).astype(BF16)
        attended_ref[:, part] = jnp.dot(
            weights, values[:, part], preferred_element_type=F32
        ).astype(BF16)

    wait(ff.at[:, pl.ds(0, 60)], ff_sent)

    @pl.when(whole)
    def _():
        wait(ff.at[:, pl.ds(0, 4)], far_sent)

    @pl.when(jnp.logical_not(whole))
    def _():
        wait(ff.at[:, pl.ds(0, 2)], far_sent)

    wait(kv.at[0, :, pl.ds(0, 63)], kv_sent)
    wait(kv.at[pl.ds(0, 3)], y_sent)

    @pl.when(holder)
    def _():
        wait(held.at[pl.ds(0, 31)], first_sent)
        wait(held.at[pl.ds(0, 63)], second_sent)

    @pl.when(jnp.logical_not(holder))
    def _():
        wait(held.at[pl.ds(0, 32)], first_sent)

    wait(arrived.at[pl.ds(0, 4)], core_sent.at[0])
    for n in range(4):
        wait(mixed.at[n], core_sent.at[n + 1])


def local(
    neighbour_rows,
    lengths,
    block_rows,
    queries,
    encoder_gain,
    weight_in,
    weight_out,
    weight_key,
    weight_value,
):
    dma = pltpu.SemaphoreType.DMA
    vmem = pl.BlockSpec(memory_space=pltpu.VMEM)
    return pl.pallas_call(
        kernel,
        out_shape=jax.ShapeDtypeStruct(queries.shape, BF16),
        in_specs=[pl.BlockSpec(memory_space=pl.ANY)] * 9,
        out_specs=vmem,
        scratch_shapes=[
            pltpu.VMEM((2, NW, 16, 896), BF16),
            pltpu.VMEM((4, 2, NW, 16, 256), BF16),
            pltpu.VMEM((8, 128, 128), BF16),
            pltpu.VMEM((NW, 16, 128), BF16),
            pltpu.VMEM((NW, 16, 128), BF16),
            pltpu.VMEM((8, 128, 128), BF16),
            pltpu.VMEM((4, 128, 256), F32),
            pltpu.VMEM((4, 128, 256), F32),
            pltpu.VMEM((NW * 16, 1), F32),
            pltpu.VMEM((1, NW * 16), F32),
            pltpu.VMEM((128, 1024), BF16),
            pltpu.VMEM((128, 1024), BF16),
            pltpu.VMEM((NW * 16, NW * 16), BF16),
            pltpu.VMEM((128, 896), BF16),
            pltpu.VMEM((1, 512), jnp.int32),
            pltpu.VMEM((2, 256), jnp.int32),
            pltpu.VMEM((256, 1024), BF16),
            pltpu.VMEM((896,), F32),
            pltpu.VMEM((14, 896), BF16),
            pltpu.VMEM((14, 896), BF16),
            pltpu.VMEM((14, 1024), BF16),
            pltpu.VMEM((14, 1024), BF16),
        ]
        + [dma((4,))] * 10
        + [dma] * 7
        + [dma((5,))] * 2
        + [dma((9,)), dma, dma],
        compiler_params=pltpu.CompilerParams(
            collective_id=0, has_side_effects=True, vmem_limit_bytes=60 * 2**20
        ),
        name="route_encode_attend",
    )(
        neighbour_rows.reshape(-1, neighbour_rows.shape[-1]),
        lengths.reshape(1, -1),
        block_rows.T,
        queries,
        encoder_gain,
        weight_in,
        weight_out.T,
        weight_key,
        weight_value,
    )


def solution(mesh):
    in_specs = (
        P(("dp", "wide"), None, None),
        P("dp"),
        P("dp", None),
        P(("dp", "wide"), "mp"),
        P(),
        P("wide", "mp"),
        P("mp", "wide"),
        P("wide", "mp"),
        P("wide", "mp"),
    )
    out_specs = P(("dp", "wide"), "mp")
    return jax.shard_map(local, mesh=mesh, in_specs=in_specs, out_specs=out_specs, check_vma=False)
```
